32 devices in a mesh: prow: 8 (over z, core), pcol: 4 (over y, x).
Axes of the slice: x: 2, y: 2, z: 4, core: 2. Of those that a mesh axis runs over, the one named last changes fastest.
Arguments:
- grace_slab: float32 [90112, 2048], P('prow', 'pcol'), may hold values from -6 to 6
- goce_slab: float32 [90112, 2048], P('prow', 'pcol'), may hold values from -6 to 240
- grace_weight: float32 [1], replicated, may hold values from 0.8 to 1.25
- goce_weight: float32 [1], replicated, may hold values from 0.8 to 1.25
- kaula_prior: float32 [2048], P('pcol'), may hold values from 2 to 20
- row_target: int32 [90112], replicated, may hold values from 0 to 90111, as said below
- column_target: int32 [2048], replicated, may hold values from 0 to 2047, as said below
Outputs:
- factored: float32 [90112, 2048], P('prow', 'pcol')
The draws below stay inside these ranges and needn't reach their ends.
Inputs may be any that keep to these rules, and one draw needn't show every extreme that they name: `row_target`: a permutation; each aligned block of 11264 entries holds exactly 1408 values in each aligned range of 11264 values. `column_target`: a permutation; each aligned block of 512 entries holds exactly 128 values in each aligned range of 512 values.
All inputs are finite; a program needn't handle non-finite values.
Results may differ from the reference program's by a relative error of at most 0.00005.
Values sent between devices are 32-bit elements; how exact they have to be, the bound alone decides.
No kernel may reach another device: no remote copies, remote signals or barrier semaphores. Data moves between devices by JAX's collectives and lax.ppermute only.
A program may use at most 256 MiB of HBM per device.

```python
import math
import jax
import jax.numpy as jnp
from jax import lax

ORDER = 90112
SLAB = 2048
PANEL = 512
BLOCK = 128
N_PROW = 8
N_PCOL = 4


def balanced_targets(key, total, groups):
    per_group = total // groups
    per_pair = per_group // groups
    first_key, second_key = jax.random.split(key)
    source_perms = jax.vmap(lambda sub_key: jax.random.permutation(sub_key, per_group))(jax.random.split(first_key, groups))
    target_perms = jax.vmap(lambda sub_key: jax.random.permutation(sub_key, per_group))(jax.random.split(second_key, groups))
    sender = jnp.broadcast_to(jnp.arange(groups, dtype=jnp.int32)[:, None], (groups, per_group))
    slot_index = jnp.broadcast_to(jnp.arange(per_group, dtype=jnp.int32)[None, :], (groups, per_group))
    receiver = slot_index // per_pair
    position = sender * per_pair + slot_index % per_pair
    values = receiver * per_group + target_perms[receiver, position]
    target_index = sender * per_group + source_perms
    return jnp.zeros((total,), jnp.int32).at[target_index.ravel()].set(values.ravel().astype(jnp.int32))


def order_positions(amount, groups):
    storage = jnp.arange(amount, dtype=jnp.int32)
    per_group = amount // groups
    local = storage % per_group
    return (local // BLOCK * groups + storage // per_group) * BLOCK + storage % BLOCK


def draw_row_target(key, part):
    return balanced_targets(key, ORDER, N_PROW)


def draw_column_target(key, part):
    return balanced_targets(key, SLAB, N_PCOL)


def draw_goce_slab(key, part):
    noise_key, diag_key = jax.random.split(jax.random.fold_in(key, 7))
    noise = jnp.clip(jax.random.normal(noise_key, (ORDER, SLAB), jnp.float32), -6.0, 6.0)
    diag_values = jax.random.uniform(diag_key, (SLAB,), jnp.float32, 120.0, 240.0)
    rows = order_positions(ORDER, N_PROW)
    cols = order_positions(SLAB, N_PCOL)
    on_diagonal = rows[:, None] == cols[None, :]
    return jnp.where(on_diagonal, diag_values[None, :], noise).astype(jnp.float32)


def level_of(rng, shape, cuts, low, high):
    def one(dim, shards_of):
        draws = jax.random.uniform(jax.random.fold_in(jax.random.fold_in(rng, 6), dim), (shards_of,), jnp.float32, low / len(cuts), high / len(cuts))
        return jnp.repeat(jnp.exp(draws), shape[dim] // shards_of).reshape((-1,) + (1,) * (len(shape) - dim - 1))

    gain = one(*cuts[0])
    for cut in cuts[1:]:
        gain = gain * one(*cut)
    return gain


def scatter_about(stream_key, dims, width, reach, pieces=(), kind=jnp.bfloat16):
    gain = level_of(stream_key, dims, pieces, -0.22, 0.18) if pieces else 1.0
    array = jax.random.normal(stream_key, dims, jnp.float32) * width * gain
    return jnp.minimum(jnp.maximum(array, -reach), reach).astype(kind)


def setup_inputs(seed: int = 0) -> dict:
    key_list = jax.random.split(jax.random.key(seed), 8)
    grace_slab = scatter_about(key_list[0], (ORDER, SLAB), 1.0, 6.0, ((0, 8), (1, 4)), jnp.float32)
    goce_slab = draw_goce_slab(jax.random.fold_in(key_list[7], 71), 0)
    grace_weight = jnp.clip(jnp.exp(jax.random.uniform(key_list[2], (1,), jnp.float32, math.log(0.8), math.log(1.25))), 0.8, 1.25)
    goce_weight = jnp.clip(jnp.exp(jax.random.uniform(key_list[3], (1,), jnp.float32, math.log(0.8), math.log(1.25))), 0.8, 1.25)
    kaula_prior = jnp.clip(jnp.exp(math.log(20.0) - 2.3025851 * jax.random.uniform(key_list[4], (SLAB,), jnp.float32) ** level_of(key_list[4], (SLAB,), ((0, 4),), -0.2, 0.2)), 2.0, 20.0)
    row_target = draw_row_target(jax.random.fold_in(key_list[7], 71), 0)
    column_target = draw_column_target(jax.random.fold_in(key_list[7], 71), 0)
    return dict(grace_slab=grace_slab, goce_slab=goce_slab, grace_weight=grace_weight, goce_weight=goce_weight, kaula_prior=kaula_prior, row_target=row_target, column_target=column_target)


def order_index(amount, groups, block_size):
    storage = jnp.arange(amount, dtype=jnp.int32)
    per_group = amount // groups
    device = storage // per_group
    local = storage % per_group
    return (local // block_size * groups + device) * block_size + local % block_size

def reference(grace_slab, goce_slab, grace_weight, goce_weight, kaula_prior, row_target, column_target):
    row_order = order_index(ORDER, N_PROW, BLOCK)
    col_order = order_index(SLAB, N_PCOL, BLOCK)
    row_storage = jnp.argsort(row_order).astype(jnp.int32)
    col_storage = jnp.argsort(col_order).astype(jnp.int32)
    input_rows = jnp.argsort(row_target).astype(jnp.int32)
    input_cols = jnp.argsort(column_target).astype(jnp.int32)
    moved = jnp.take(jnp.take(grace_slab, jnp.take(input_rows, row_storage), axis=0), jnp.take(input_cols, col_storage), axis=1)
    goce_order = jnp.take(jnp.take(goce_slab, row_storage, axis=0), col_storage, axis=1)
    kaula_order = jnp.take(kaula_prior, col_storage)
    combined = grace_weight[0] * moved + goce_weight[0] * goce_order
    diag_index = jnp.arange(SLAB, dtype=jnp.int32)
    combined = combined.at[diag_index, diag_index].add(kaula_order)
    diag_block = combined[:PANEL, :PANEL]
    symmetric = jnp.tril(diag_block) + jnp.tril(diag_block, -1).T
    factor = jnp.linalg.cholesky(symmetric)
    inverse = jax.scipy.linalg.solve_triangular(factor, jnp.eye(PANEL, dtype=jnp.float32), lower=True)
    factors = jnp.dot(combined[:, :PANEL], inverse.T, precision=lax.Precision.HIGHEST)
    factors = factors.at[:PANEL].set(factor)
    update = combined[:, PANEL:] - jnp.dot(factors, factors[PANEL:SLAB].T, precision=lax.Precision.HIGHEST)
    update = update.at[:PANEL].set(combined[:PANEL, PANEL:])
    result_order = jnp.concatenate([factors, update], axis=1)
    return jnp.take(jnp.take(result_order, row_order, axis=0), col_order, axis=1)
```

```python
import functools

import jax
import jax.numpy as jnp
from jax import lax
from jax.experimental import pallas as pl
from jax.experimental.pallas import tpu as pltpu
from jax.sharding import PartitionSpec as P

SLAB = 2048
PANEL = 512
BLOCK = 128
LANES = 128
SUBLANES = 8
VMEM_LIMIT = 56 * 1024 * 1024


def order_index(amount, device, groups, block_size):
    local = jnp.arange(amount, dtype=jnp.int32)
    return (local // block_size * groups + device) * block_size + local % block_size


def group_step(groups, width, most=1024):
    best = 1
    for size in range(1, groups + 1):
        if groups % size == 0 and size * width <= most:
            best = size
    return best


def chunk_widths(total, head):
    rest = total - head
    widths = [head]
    for part in (rest // 3, rest // 3, 2 * rest // 9):
        widths.append(part // 16 * 16)
    widths.append(total - sum(widths))
    return widths


def row_view(array):
    rows, cols = array.shape
    tiles = cols // LANES
    shaped = array.reshape(rows // SUBLANES, SUBLANES, tiles, LANES)
    return shaped.transpose(0, 2, 1, 3).reshape(rows * tiles, LANES)


def view_base(index, tiles):
    return index // SUBLANES * (SUBLANES * tiles) + index % SUBLANES


def split(value):
    high = value.astype(jnp.bfloat16)
    low = (value - high.astype(jnp.float32)).astype(jnp.bfloat16)
    return high, low


def split_array(value):
    high = lax.reduce_precision(value, 8, 7)
    return high.astype(jnp.bfloat16), (value - high).astype(jnp.bfloat16)


def product(left, right):
    return jnp.dot(left, right, preferred_element_type=jnp.float32)


def copy_rows(index_ref, first, source, target, count, tiles):
    def move(step, carry):
        for lane in range(SUBLANES):
            base = index_ref[first + step * SUBLANES + lane]
            target[pl.ds(step * SUBLANES * tiles + lane, tiles, stride=SUBLANES), :] = source[
                pl.ds(base, tiles, stride=SUBLANES), :
            ]
        return carry

    lax.fori_loop(0, count // SUBLANES, move, 0, unroll=4)


def from_view(value, rows, tiles):
    shaped = value.reshape(rows // SUBLANES, tiles, SUBLANES, LANES)
    return jnp.concatenate([shaped[:, t].reshape(rows, LANES) for t in range(tiles)], axis=1)


def pack_kernel(chunks, tiles, direct, index_ref, source_hbm, onehot_ref, *refs):
    outs = refs[: len(chunks)]
    held, picked, sem = refs[len(chunks) :]
    step = pl.program_id(0)

    @pl.when(step == 0)
    def _():
        copy = pltpu.make_async_copy(source_hbm, held, sem)
        copy.start()
        copy.wait()

    for (first_step, steps, first_row, groups, width), out_ref in zip(chunks, outs):

        @pl.when((step >= first_step) & (step < first_step + steps))
        def _():
            rows = groups * width
            first = first_row + (step - first_step) * rows
            copy_rows(index_ref, first, held, picked, rows, tiles)
            high, low = split(from_view(picked[: rows * tiles], rows, tiles))
            moved = product(high, onehot_ref[...]) + product(low, onehot_ref[...])
            if direct:
                lanes = out_ref.shape[3]
                for c in range(out_ref.shape[1]):
                    part = moved[:, c * lanes : (c + 1) * lanes]
                    out_ref[:, c] = part.reshape(groups, width, lanes)
            else:
                out_ref[...] = moved.reshape(groups, width, moved.shape[1])


def chunk_map(first_step, steps, zeros, step):
    return (jnp.clip(step - first_step, 0, steps - 1),) + (0,) * zeros


def pack(view, bases, onehot, row_devices, col_devices, widths):
    cols = onehot.shape[0]
    tiles = cols // LANES
    group = cols // col_devices
    direct = group % LANES == 0
    chunks, shapes, specs, first_step, first_row = [], [], [], 0, 0
    for width in widths:
        groups = group_step(row_devices, width)
        steps = row_devices // groups
        chunks.append((first_step, steps, first_row, groups, width))
        inner = (col_devices, width, group) if direct else (width, cols)
        shapes.append(jax.ShapeDtypeStruct((row_devices,) + inner, jnp.float32))
        place = functools.partial(chunk_map, first_step, steps, len(inner))
        specs.append(pl.BlockSpec((groups,) + inner, place))
        first_step += steps
        first_row += row_devices * width
    most = max(groups * width for _, _, _, groups, width in chunks)
    outs = pl.pallas_call(
        functools.partial(pack_kernel, tuple(chunks), tiles, direct),
        out_shape=shapes,
        grid=(first_step,),
        in_specs=[
            pl.BlockSpec(memory_space=pltpu.SMEM),
            pl.BlockSpec(memory_space=pl.ANY),
            pl.BlockSpec((cols, cols), lambda i: (0, 0)),
        ],
        out_specs=specs,
        scratch_shapes=[
            pltpu.VMEM(view.shape, jnp.float32),
            pltpu.VMEM((most * tiles, LANES), jnp.float32),
            pltpu.SemaphoreType.DMA,
        ],
        compiler_params=pltpu.CompilerParams(vmem_limit_bytes=VMEM_LIMIT),
        cost_estimate=pl.CostEstimate(
            flops=4 * first_row * cols * cols,
            bytes_accessed=4 * view.size + 24 * first_row * cols,
            transcendentals=0,
        ),
        name="pack",
    )(bases, view, onehot)
    packets = []
    for out, width in zip(outs, widths):
        if not direct:
            out = out.reshape(row_devices, width, col_devices, group).transpose(0, 2, 1, 3)
        packets.append(out.reshape(row_devices * col_devices, width, group))
    return packets


def arrived_spec(received, groups):
    shape = (groups,) + received.shape[1:]
    return pl.BlockSpec(shape, lambda i: (i,) + (0,) * (len(shape) - 1))


def load_arrived(ref):
    if len(ref.shape) == 4:
        groups, devices, width, lanes = ref.shape
        parts = [ref[:, c].reshape(groups * width, lanes) for c in range(devices)]
        return jnp.concatenate(parts, axis=1)
    groups, width, lanes = ref.shape
    return ref[...].reshape(groups * width, lanes)


def panel_kernel(rows, index_ref, weight_ref, received_ref, onehot_ref, goce_hbm, out_ref, held, picked, sem):
    step = pl.program_id(0)

    @pl.when(step == 0)
    def _():
        copy = pltpu.make_async_copy(goce_hbm.at[:, pl.ds(0, BLOCK)], held, sem)
        copy.start()
        copy.wait()

    copy_rows(index_ref, step * rows, held, picked, rows, 1)
    high, low = split(load_arrived(received_ref))
    moved = product(high, onehot_ref[...]) + product(low, onehot_ref[...])
    out_ref[...] = weight_ref[0] * moved + weight_ref[1] * picked[...]


def panel_part(received, places, weights, onehot, goce):
    row_devices, width = received.shape[0], received.shape[-2]
    cols = onehot.shape[0]
    groups = group_step(row_devices, width)
    rows = groups * width
    return pl.pallas_call(
        functools.partial(panel_kernel, rows),
        out_shape=jax.ShapeDtypeStruct((row_devices * width, BLOCK), jnp.float32),
        grid=(row_devices // groups,),
        in_specs=[
            pl.BlockSpec(memory_space=pltpu.SMEM),
            pl.BlockSpec(memory_space=pltpu.SMEM),
            arrived_spec(received, groups),
            pl.BlockSpec((cols, BLOCK), lambda i: (0, 0)),
            pl.BlockSpec(memory_space=pl.ANY),
        ],
        out_specs=pl.BlockSpec((rows, BLOCK), lambda i: (i, 0)),
        scratch_shapes=[
            pltpu.VMEM((goce.shape[0], BLOCK), jnp.float32),
            pltpu.VMEM((rows, BLOCK), jnp.float32),
            pltpu.SemaphoreType.DMA,
        ],
        compiler_params=pltpu.CompilerParams(vmem_limit_bytes=VMEM_LIMIT),
        cost_estimate=pl.CostEstimate(
            flops=4 * row_devices * width * cols * BLOCK,
            bytes_accessed=4 * goce.shape[0] * BLOCK + 16 * row_devices * width * cols,
            transcendentals=0,
        ),
        name="panel",
    )(places, weights, received, onehot, goce)


def update_kernel(masked, weight_ref, received_ref, raw_ref, keep_ref, onehot_ref, high_ref, low_ref, out_ref):
    panels = high_ref.shape[0] // BLOCK
    raw = jnp.concatenate([raw_ref[p] for p in range(panels)], axis=1)
    if masked:
        raw = raw * keep_ref[...]
    high, low = split(raw)
    total = product(high, high_ref[...]) + product(low, high_ref[...]) + product(high, low_ref[...])
    high, low = split(load_arrived(received_ref))
    moved = product(high, onehot_ref[...]) + product(low, onehot_ref[...])
    total = total + weight_ref[0] * moved
    rows, cols = total.shape
    for t in range(cols // LANES):
        out_ref[:, t] = total[:, t * LANES : (t + 1) * LANES].reshape(rows // SUBLANES, SUBLANES, LANES)


def update_part(received, raw, keep, weights, onehot, high, low, masked):
    row_devices, width = received.shape[0], received.shape[-2]
    cols = onehot.shape[0]
    tiles = cols // LANES
    groups = group_step(row_devices, width)
    rows = groups * width
    total = row_devices * width
    return pl.pallas_call(
        functools.partial(update_kernel, masked),
        out_shape=jax.ShapeDtypeStruct((total // SUBLANES, tiles, SUBLANES, LANES), jnp.float32),
        grid=(total // rows,),
        in_specs=[
            pl.BlockSpec(memory_space=pltpu.SMEM),
            arrived_spec(received, groups),
            pl.BlockSpec((PANEL // BLOCK, rows, BLOCK), lambda i: (0, i, 0)),
            pl.BlockSpec((rows, 1), (lambda i: (i, 0)) if masked else (lambda i: (0, 0))),
            pl.BlockSpec(onehot.shape, lambda i: (0, 0)),
            pl.BlockSpec(high.shape, lambda i: (0, 0)),
            pl.BlockSpec(low.shape, lambda i: (0, 0)),
        ],
        out_specs=pl.BlockSpec((rows // SUBLANES, tiles, SUBLANES, LANES), lambda i: (i, 0, 0, 0)),
        compiler_params=pltpu.CompilerParams(vmem_limit_bytes=VMEM_LIMIT),
        cost_estimate=pl.CostEstimate(
            flops=2 * total * cols * (3 * PANEL + 2 * cols),
            bytes_accessed=4 * total * (2 * cols + PANEL),
            transcendentals=0,
        ),
        name="update",
    )(weights, received, raw, keep, onehot, high, low)


def finish_kernel(rows, tiles, has_head, bounds_ref, index_ref, part_hbm, head_ref, base_hbm, out_hbm, held, picked, before, after, part_sem, in_sem, out_sem):
    size = part_hbm.shape[0]
    first, last = bounds_ref[0], bounds_ref[1]
    for source in range(1, bounds_ref.shape[0] // 2):
        first = jnp.minimum(first, bounds_ref[2 * source])
        last = jnp.maximum(last, bounds_ref[2 * source + 1])
    first = first // rows
    steps = last // rows + 1 - first

    def block(step):
        return pl.ds(pl.multiple_of((first + step) * rows, rows), rows)

    def fetch(step, slot):
        return pltpu.make_async_copy(out_hbm.at[block(step)], before.at[slot], in_sem.at[slot])

    def store(step, slot):
        return pltpu.make_async_copy(after.at[slot], out_hbm.at[block(step)], out_sem.at[slot])

    part_copy = pltpu.make_async_copy(part_hbm, held.at[pl.ds(0, size)], part_sem)
    part_copy.start()
    fetch(0, 0).start()
    held[pl.ds(size, SUBLANES * tiles), :] = jnp.zeros((SUBLANES * tiles, LANES), jnp.float32)
    part_copy.wait()

    def body(step, carry):
        slot = lax.rem(step, 2)

        @pl.when(step + 1 < steps)
        def _():
            fetch(step + 1, 1 - slot).start()

        copy_rows(index_ref, (first + step) * rows, held, picked, rows, tiles)
        fetch(step, slot).wait()

        @pl.when(step >= 2)
        def _():
            store(step - 2, slot).wait()

        after[slot] = before[slot] + from_view(picked[...], rows, tiles)
        if has_head:

            @pl.when(step == 0)
            def _():
                count = head_ref.shape[0]
                after[0, :count] = after[0, :count] + head_ref[...]

        store(step, slot).start()
        return carry

    lax.fori_loop(0, steps, body, 0)

    @pl.when(steps >= 2)
    def _():
        store(steps - 2, lax.rem(steps, 2)).wait()

    store(steps - 1, lax.rem(steps + 1, 2)).wait()


def finish_part(base, part, bounds, positions, offset, head, has_head):
    total, cols = base.shape
    tiles = cols // LANES
    rows = head.shape[0]
    while rows < 512 and total % (2 * rows) == 0:
        rows *= 2
    count = part.shape[0] // tiles
    local = positions - offset
    index = jnp.where((local >= 0) & (local < count), local, count)
    return pl.pallas_call(
        functools.partial(finish_kernel, rows, tiles, has_head),
        out_shape=jax.ShapeDtypeStruct((total, cols), jnp.float32),
        in_specs=[
            pl.BlockSpec(memory_space=pltpu.SMEM),
            pl.BlockSpec(memory_space=pltpu.SMEM),
            pl.BlockSpec(memory_space=pl.ANY),
            pl.BlockSpec(memory_space=pltpu.VMEM),
            pl.BlockSpec(memory_space=pl.ANY),
        ],
        out_specs=pl.BlockSpec(memory_space=pl.ANY),
        scratch_shapes=[
            pltpu.VMEM((part.shape[0] + SUBLANES * tiles, LANES), jnp.float32),
            pltpu.VMEM((rows * tiles, LANES), jnp.float32),
            pltpu.VMEM((2, rows, cols), jnp.float32),
            pltpu.VMEM((2, rows, cols), jnp.float32),
            pltpu.SemaphoreType.DMA,
            pltpu.SemaphoreType.DMA((2,)),
            pltpu.SemaphoreType.DMA((2,)),
        ],
        input_output_aliases={4: 0},
        compiler_params=pltpu.CompilerParams(vmem_limit_bytes=VMEM_LIMIT),
        cost_estimate=pl.CostEstimate(
            flops=2 * count * cols, bytes_accessed=16 * count * cols, transcendentals=0
        ),
        name="finish",
    )(bounds, view_base(index, tiles), part, head, base)


def precise(left, right):
    return jnp.dot(left, right, precision=lax.Precision.HIGHEST)


def cholesky_inverse(blocks, pause):
    count = len(blocks)
    size = blocks[0][0].shape[0]
    identity = jnp.eye(size, dtype=jnp.float32)
    factor, inverse = {}, {}
    for b in range(count):
        pivot = jnp.tril(blocks[b][b]) + jnp.tril(blocks[b][b], -1).T
        if b:
            left = jnp.concatenate([factor[b, k] for k in range(b)], axis=1)
            pivot = pivot - precise(left, left.T)
        factor[b, b] = jnp.linalg.cholesky(pivot, symmetrize_input=False)
        inverse[b, b] = jax.scipy.linalg.solve_triangular(factor[b, b], identity, lower=True)
        if b + 1 < count:
            below = jnp.concatenate([blocks[i][b] for i in range(b + 1, count)], axis=0)
            if b:
                rows = [
                    jnp.concatenate([factor[i, k] for k in range(b)], axis=1)
                    for i in range(b + 1, count)
                ]
                below = below - precise(jnp.concatenate(rows, axis=0), left.T)
            below = pause(b, precise(below, inverse[b, b].T))
            for i in range(b + 1, count):
                factor[i, b] = below[(i - b - 1) * size : (i - b) * size]
    zero = jnp.zeros((size, size), jnp.float32)
    for b in range(1, count):
        left = jnp.concatenate([factor[b, k] for k in range(b)], axis=1)
        above = [
            jnp.concatenate([inverse[k, j] if k >= j else zero for j in range(b)], axis=1)
            for k in range(b)
        ]
        solved = -precise(inverse[b, b], precise(left, jnp.concatenate(above, axis=0)))
        for j in range(b):
            inverse[b, j] = solved[:, j * size : (j + 1) * size]
    whole = [
        [
            jnp.concatenate([part[i, j] if i >= j else zero for j in range(count)], axis=1)
            for i in range(count)
        ]
        for part in (factor, inverse)
    ]
    return jnp.concatenate(whole[0], axis=0), jnp.concatenate(whole[1], axis=0)


def shards(
    grace_slab, goce_slab, grace_weight, goce_weight, kaula_prior, row_target, column_target
):
    row_devices = lax.axis_size("prow")
    col_devices = lax.axis_size("pcol")
    row_id = lax.axis_index("prow")
    col_id = lax.axis_index("pcol")
    rows_here, cols_here = grace_slab.shape
    tiles = cols_here // LANES
    row_group = rows_here // row_devices
    col_group = cols_here // col_devices
    per_device = SLAB // (BLOCK * row_devices)
    lead = per_device * BLOCK
    widths = chunk_widths(row_group, lead)
    starts = [sum(widths[:n]) for n in range(len(widths))]
    weights = jnp.concatenate([grace_weight, goce_weight])

    bits = (rows_here - 1).bit_length()
    mask = (1 << bits) - 1
    local = jnp.arange(rows_here, dtype=jnp.int32)
    mine = lax.dynamic_slice_in_dim(row_target, row_id * rows_here, rows_here)
    sources = (jnp.sort(mine * (1 << bits) + local) & mask).reshape(row_devices, row_group)
    source_bases = view_base(sources, tiles)
    my_cols = lax.dynamic_slice_in_dim(column_target, col_id * cols_here, cols_here)
    col_places = jnp.sum((my_cols[None, :] < my_cols[:, None]).astype(jnp.int32), axis=1)
    col_iota = jnp.arange(cols_here, dtype=jnp.int32)
    send_onehot = (col_places[:, None] == col_iota[None, :]).astype(jnp.bfloat16)

    view = row_view(grace_slab)
    chunk_bases = [
        source_bases[:, start : start + width].reshape(-1) for start, width in zip(starts, widths)
    ]
    packets = pack(view, chunk_bases[0], send_onehot, row_devices, col_devices, widths[:1])
    packets += pack(
        view, jnp.concatenate(chunk_bases[1:]), send_onehot, row_devices, col_devices, widths[1:]
    )

    sorted_rows = jnp.sort(row_target.reshape(row_devices, rows_here), axis=1)
    places = lax.dynamic_slice_in_dim(sorted_rows, row_id * row_group, row_group, axis=1)
    places = places - row_id * rows_here
    chunk_places = [
        places[:, start : start + width].reshape(-1) for start, width in zip(starts, widths)
    ]
    positions = jnp.sort(jnp.concatenate(chunk_places) * (1 << bits) + local) & mask
    sorted_cols = jnp.sort(column_target.reshape(col_devices, cols_here), axis=1)
    col_targets = lax.dynamic_slice_in_dim(sorted_cols, col_id * col_group, col_group, axis=1)
    col_targets = col_targets.reshape(-1) - col_id * cols_here
    take_onehot = (col_targets[:, None] == col_iota[None, :]).astype(jnp.bfloat16)
    order_cols = order_index(cols_here, col_id, col_devices, BLOCK)
    in_panel = order_cols < PANEL
    rest_onehot = jnp.where(in_panel[None, :], jnp.zeros((), jnp.bfloat16), take_onehot)
    scale = jnp.where(in_panel, 0.0, goce_weight[0]).astype(jnp.float32)
    out = goce_slab * scale[None, :]

    def exchange(packet):
        got = lax.all_to_all(packet, ("prow", "pcol"), split_axis=0, concat_axis=0, tiled=True)
        got = got.reshape(row_devices, col_devices, packet.shape[1], col_group)
        if col_group % LANES:
            got = got.transpose(0, 2, 1, 3).reshape(row_devices, packet.shape[1], cols_here)
        return got

    received = {0: exchange(packets[0])}
    panels, raws = {}, {}
    places_ends = jnp.stack(
        [places[:, jnp.array(starts)], places[:, jnp.array([s + w - 1 for s, w in zip(starts, widths)])]],
        axis=-1,
    )
    ends = [places_ends[:, n].reshape(-1) for n in range(len(widths))]

    def begin(n, after):
        packet, after, received[n - 1] = lax.optimization_barrier(
            (packets[n], after, received[n - 1])
        )
        received[n] = exchange(packet)
        return after

    def gather(n):
        panels[n] = panel_part(
            received[n], chunk_places[n], weights, take_onehot[:, :BLOCK], goce_slab
        )
        raws[n] = lax.all_gather(panels[n], "pcol", axis=0)

    all_kaula = lax.all_gather(kaula_prior[:BLOCK], "pcol", axis=0)
    chunk_places, positions, take_onehot, rest_onehot, ends, out, packets[2:], all_kaula = begin(
        1, (chunk_places, positions, take_onehot, rest_onehot, ends, out, packets[2:], all_kaula)
    )
    gather(0)
    my_lead = jnp.take(panels[0], positions[:lead], axis=0)
    lead_all = lax.all_gather(my_lead, ("prow", "pcol"), axis=0)
    lead_all = lead_all.reshape(row_devices, col_devices, per_device, BLOCK, BLOCK)

    def lead_block(row, col):
        return lead_all[row % row_devices, col, row // row_devices]

    panel_blocks = PANEL // BLOCK
    blocks = [
        [
            lead_block(i, j) + (jnp.diag(all_kaula[i]) if i == j else 0.0)
            for j in range(i + 1)
        ]
        for i in range(panel_blocks)
    ]

    def pause(step, value):
        if step == 0:
            value = begin(2, value)
            gather(1)
        return value

    factor, inverse = cholesky_inverse(blocks, pause)
    col_rows = []
    for n in range(cols_here // BLOCK):
        block = n * col_devices + col_id
        rows = lax.dynamic_index_in_dim(lead_all, block % row_devices, 0, keepdims=False)
        rows = lax.dynamic_index_in_dim(rows, block // row_devices, 1, keepdims=False)
        col_rows.append(rows[:panel_blocks].transpose(1, 0, 2).reshape(BLOCK, PANEL))
    col_rows = jnp.concatenate(col_rows, axis=0)
    solved = precise(inverse, col_rows.T)
    panel_iota = jnp.arange(PANEL, dtype=jnp.int32)
    identity = (panel_iota[:, None] == order_cols[None, :]).astype(jnp.float32)
    matrix = precise(inverse.T, jnp.where(in_panel[None, :], identity, -solved))
    matrix_high, matrix_low = split_array(matrix)

    order_rows = order_index(lead, row_id, row_devices, BLOCK)
    on_diagonal = order_rows[:, None] == order_cols[None, :]
    known = jnp.take(
        jnp.take(factor, jnp.minimum(order_rows, PANEL - 1), axis=0),
        jnp.minimum(order_cols, PANEL - 1),
        axis=1,
    )
    in_block = (order_rows[:, None] < PANEL) & in_panel[None, :]
    head = jnp.where(in_block, known, jnp.where(on_diagonal, kaula_prior[None, :], 0.0))
    first = chunk_places[0]
    first_order = (first // BLOCK * row_devices + row_id) * BLOCK + first % BLOCK
    keep = jnp.where(first_order < PANEL, 0.0, 1.0)[:, None].astype(jnp.float32)

    offset = 0
    last = len(widths) - 1
    for n in range(len(widths)):
        if n == last - 1:
            received[last], out = lax.optimization_barrier((received[last], out))
            gather(last)
        part = update_part(
            received[n], raws[n], keep, weights, rest_onehot, matrix_high, matrix_low, masked=n == 0
        ).reshape(-1, LANES)
        out = finish_part(out, part, ends[n], positions, offset, head, has_head=n == 0)
        offset += part.shape[0] // tiles
        if n + 3 <= last:
            out = begin(n + 3, out)
            gather(n + 2)
    return out


def solution(mesh):
    return jax.shard_map(
        shards,
        mesh=mesh,
        in_specs=(P("prow", "pcol"), P("prow", "pcol"), P(), P(), P("pcol"), P(), P()),
        out_specs=P("prow", "pcol"),
        check_vma=False,
    )
```

```python
import functools

import jax
import jax.numpy as jnp
from jax import lax
from jax.experimental import pallas as pl
from jax.experimental.pallas import tpu as pltpu
from jax.sharding import PartitionSpec as P

SLAB = 2048
PANEL = 512
BLOCK = 128
LANES = 128
SUBLANES = 8
LIGHT = pl.CostEstimate(flops=1, bytes_accessed=1, transcendentals=0)
HEAVY = pl.CostEstimate(flops=1, bytes_accessed=700_000_000, transcendentals=0)
VMEM_LIMIT = 56 * 1024 * 1024


def order_index(amount, device, groups, block_size):
    local = jnp.arange(amount, dtype=jnp.int32)
    return (local // block_size * groups + device) * block_size + local % block_size


def group_step(groups, width, most=1024):
    best = 1
    for size in range(1, groups + 1):
        if groups % size == 0 and size * width <= most:
            best = size
    return best


def chunk_widths(total, head):
    first = max(head, total * 7 // 22 // 16 * 16)
    second = min(total - first, total * 25 // 88) // 16 * 16
    return first, second, total - first - second


def row_view(array):
    rows, cols = array.shape
    tiles = cols // LANES
    shaped = array.reshape(rows // SUBLANES, SUBLANES, tiles, LANES)
    return shaped.transpose(0, 2, 1, 3).reshape(rows * tiles, LANES)


def view_base(index, tiles):
    return index // SUBLANES * (SUBLANES * tiles) + index % SUBLANES


def split(value):
    high = value.astype(jnp.bfloat16)
    low = (value - high.astype(jnp.float32)).astype(jnp.bfloat16)
    return high, low


def split_array(value):
    high = lax.reduce_precision(value, 8, 7)
    return high.astype(jnp.bfloat16), (value - high).astype(jnp.bfloat16)


def product(left, right):
    return jnp.dot(left, right, preferred_element_type=jnp.float32)


def copy_rows(index_ref, first, source, target, count, tiles, stride):
    def move(step, carry):
        for lane in range(SUBLANES):
            base = index_ref[first + step * SUBLANES + lane]
            target[pl.ds(step * SUBLANES * tiles + lane, tiles, stride=SUBLANES), :] = source[
                pl.ds(base, tiles, stride=stride), :
            ]
        return carry

    lax.fori_loop(0, count // SUBLANES, move, 0, unroll=4)


def from_view(value, rows, tiles):
    shaped = value.reshape(rows // SUBLANES, tiles, SUBLANES, LANES)
    return jnp.concatenate([shaped[:, t].reshape(rows, LANES) for t in range(tiles)], axis=1)


def pack_kernel(rows, tiles, index_ref, source_hbm, onehot_ref, *refs):
    outs, (held, picked, sem) = refs[:-3], refs[-3:]
    step = pl.program_id(0)

    @pl.when(step == 0)
    def _():
        copy = pltpu.make_async_copy(source_hbm, held, sem)
        copy.start()
        copy.wait()

    copy_rows(index_ref, step * rows, held, picked, rows, tiles, SUBLANES)
    high, low = split(from_view(picked[...], rows, tiles))
    places = [(out, None) for out in outs]
    if len(outs) == 1:
        places = [(outs[0], d) for d in range(outs[0].shape[1])]
    lanes = onehot_ref.shape[2]
    if lanes % LANES == 0:
        whole = jnp.concatenate([onehot_ref[d] for d in range(len(places))], axis=1)
        moved = product(high, whole) + product(low, whole)
        parts = [moved[:, d * lanes : (d + 1) * lanes] for d in range(len(places))]
    else:
        parts = [
            product(high, onehot_ref[d]) + product(low, onehot_ref[d]) for d in range(len(places))
        ]
    for part, (out, d) in zip(parts, places):
        if d is None:
            out[...] = part.reshape(out.shape)
        else:
            out[:, d] = part.reshape(out.shape[0], out.shape[2], lanes)


def pack(view, bases, onehot, row_devices, width, apart):
    col_devices, cols, group = onehot.shape
    tiles = cols // LANES
    groups = group_step(row_devices, width)
    rows = groups * width
    if apart:
        shapes = [jax.ShapeDtypeStruct((row_devices, width, group), jnp.float32)] * col_devices
        specs = [pl.BlockSpec((groups, width, group), lambda i: (i, 0, 0))] * col_devices
    else:
        shapes = [jax.ShapeDtypeStruct((row_devices, col_devices, width, group), jnp.float32)]
        specs = [pl.BlockSpec((groups, col_devices, width, group), lambda i: (i, 0, 0, 0))]
    return pl.pallas_call(
        functools.partial(pack_kernel, rows, tiles),
        out_shape=shapes,
        grid=(row_devices // groups,),
        in_specs=[
            pl.BlockSpec(memory_space=pltpu.SMEM),
            pl.BlockSpec(memory_space=pl.ANY),
            pl.BlockSpec(onehot.shape, lambda i: (0, 0, 0)),
        ],
        out_specs=specs,
        scratch_shapes=[
            pltpu.VMEM(view.shape, jnp.float32),
            pltpu.VMEM((rows * tiles, LANES), jnp.float32),
            pltpu.SemaphoreType.DMA,
        ],
        compiler_params=pltpu.CompilerParams(vmem_limit_bytes=VMEM_LIMIT),
        cost_estimate=LIGHT,
        name="pack",
    )(bases, view, onehot)


def place_columns(pieces, onehot_ref, rows):
    if len(pieces[0].shape) == 4:
        pieces = [pieces[0][:, c] for c in range(pieces[0].shape[1])]
    values = [piece[...].reshape(rows, piece.shape[-1]) for piece in pieces]
    if values[0].shape[1] % LANES == 0:
        high, low = split(jnp.concatenate(values, axis=1))
        whole = onehot_ref[...].reshape(high.shape[1], onehot_ref.shape[2])
        return product(high, whole) + product(low, whole)
    total = None
    for d, value in enumerate(values):
        high, low = split(value)
        part = product(high, onehot_ref[d]) + product(low, onehot_ref[d])
        total = part if total is None else total + part
    return total


def mix_kernel(rows, counts, onehot_ref, *refs):
    pieces, outs = refs[: -len(counts)], refs[-len(counts) :]
    moved = place_columns(pieces, onehot_ref, rows)
    tile = 0
    for count, out in zip(counts, outs):
        for t in range(count):
            part = moved[:, (tile + t) * LANES : (tile + t + 1) * LANES]
            out[:, t] = part.reshape(out.shape[0], out.shape[2], LANES)
        tile += count


def mix(pieces, onehot, counts):
    row_devices, width, lanes = pieces[0].shape
    groups = group_step(row_devices, width)
    rows = groups * width
    return pl.pallas_call(
        functools.partial(mix_kernel, rows, counts),
        out_shape=[
            jax.ShapeDtypeStruct((row_devices, count, width, LANES), jnp.float32) for count in counts
        ],
        grid=(row_devices // groups,),
        in_specs=[pl.BlockSpec(onehot.shape, lambda i: (0, 0, 0))]
        + [pl.BlockSpec((groups, width, lanes), lambda i: (i, 0, 0))] * len(pieces),
        out_specs=[
            pl.BlockSpec((groups, count, width, LANES), lambda i: (i, 0, 0, 0)) for count in counts
        ],
        compiler_params=pltpu.CompilerParams(vmem_limit_bytes=VMEM_LIMIT),
        cost_estimate=LIGHT,
        name="mix",
    )(onehot, *pieces)


def goce_rows_kernel(rows, index_ref, weight_ref, goce_hbm, out_ref, held, picked, sem):
    step = pl.program_id(0)

    @pl.when(step == 0)
    def _():
        copy = pltpu.make_async_copy(goce_hbm.at[:, pl.ds(0, BLOCK)], held, sem)
        copy.start()
        copy.wait()

    copy_rows(index_ref, step * rows, held, picked, rows, 1, 1)
    out_ref[...] = weight_ref[1] * picked[...]


def goce_rows(places, weights, goce, row_devices):
    total = places.shape[0]
    rows = total // row_devices * group_step(row_devices, total // row_devices)
    return pl.pallas_call(
        functools.partial(goce_rows_kernel, rows),
        out_shape=jax.ShapeDtypeStruct((total, BLOCK), jnp.float32),
        grid=(total // rows,),
        in_specs=[
            pl.BlockSpec(memory_space=pltpu.SMEM),
            pl.BlockSpec(memory_space=pltpu.SMEM),
            pl.BlockSpec(memory_space=pl.ANY),
        ],
        out_specs=pl.BlockSpec((rows, BLOCK), lambda i: (i, 0)),
        scratch_shapes=[
            pltpu.VMEM((goce.shape[0], BLOCK), jnp.float32),
            pltpu.VMEM((rows, BLOCK), jnp.float32),
            pltpu.SemaphoreType.DMA,
        ],
        compiler_params=pltpu.CompilerParams(vmem_limit_bytes=VMEM_LIMIT),
        cost_estimate=LIGHT,
        name="goce_rows",
    )(places, weights, goce)


def panel_kernel(rows, weight_ref, added_ref, onehot_ref, received_ref, out_ref):
    moved = place_columns([received_ref], onehot_ref, rows)
    out_ref[...] = weight_ref[0] * moved + added_ref[...]


def panel_part(received, added, weights, onehot):
    row_devices, width = received.shape[0], received.shape[2]
    groups = group_step(row_devices, width)
    rows = groups * width
    return pl.pallas_call(
        functools.partial(panel_kernel, rows),
        out_shape=jax.ShapeDtypeStruct((row_devices * width, BLOCK), jnp.float32),
        grid=(row_devices // groups,),
        in_specs=[
            pl.BlockSpec(memory_space=pltpu.SMEM),
            pl.BlockSpec((rows, BLOCK), lambda i: (i, 0)),
            pl.BlockSpec(onehot.shape, lambda i: (0, 0, 0)),
            pl.BlockSpec((groups,) + received.shape[1:], lambda i: (i, 0, 0, 0)),
        ],
        out_specs=pl.BlockSpec((rows, BLOCK), lambda i: (i, 0)),
        compiler_params=pltpu.CompilerParams(vmem_limit_bytes=VMEM_LIMIT),
        cost_estimate=HEAVY,
        name="panel",
    )(weights, added, onehot, received)


def update_kernel(rows, placed, parts, weight_ref, mask_ref, keep_ref, high_ref, low_ref, *refs):
    step = pl.program_id(0)
    raw_count = sum(count for _, _, count in parts)
    raws, arrays, out_ref = refs[:raw_count], refs[raw_count:-1], refs[-1]

    def compute(pieces):
        raw = jnp.concatenate(pieces, axis=1)
        if not placed:
            raw = raw * keep_ref[...]
        high, low = split(raw)
        total = product(high, high_ref[...]) + product(low, high_ref[...])
        total = total + product(high, low_ref[...])
        if placed:
            shape = arrays[0].shape
            tiles = [arrays[0][:, t].reshape(rows, LANES) for t in range(shape[1])]
        else:
            moved = place_columns(arrays[1:], arrays[0], rows)
            tiles = [moved[:, t * LANES : (t + 1) * LANES] for t in range(moved.shape[1] // LANES)]
        for t in range(total.shape[1] // LANES):
            lanes = slice(t * LANES, (t + 1) * LANES)
            part = total[:, lanes]
            if t < len(tiles):
                part = part + (weight_ref[0] * mask_ref[:, lanes]) * tiles[t]
            out_ref[:, t] = part.reshape(rows // SUBLANES, SUBLANES, LANES)

    used = 0
    for first, steps, count in parts:
        mine = raws[used : used + count]
        used += count

        @pl.when((step >= first) & (step < first + steps))
        def _():
            if count == 1:
                compute([mine[0][p] for p in range(high_ref.shape[0] // BLOCK)])
            else:
                compute([ref[...] for ref in mine])


def part_map(first, steps, step):
    return (jnp.clip(step - first, 0, steps - 1), 0)


def update_part(arrays, raw, keep, weights, mask, onehot, high, low):
    placed = onehot is None
    row_devices, width, lanes = arrays[0].shape[0], arrays[0].shape[-2], arrays[0].shape[-1]
    cols = high.shape[1]
    tiles = cols // LANES
    groups = group_step(row_devices, width)
    rows = groups * width
    total = row_devices * width
    if isinstance(raw, list):
        parts, raw_specs, flat, first = [], [], [], 0
        for pieces in raw:
            steps = pieces[0].shape[0] // rows
            parts.append((first, steps, len(pieces)))
            place = functools.partial(part_map, first, steps)
            raw_specs += [pl.BlockSpec((rows, BLOCK), place)] * len(pieces)
            flat += pieces
            first += steps
    else:
        parts = [(0, row_devices // groups, 1)]
        raw_specs = [pl.BlockSpec((high.shape[0] // BLOCK, rows, BLOCK), lambda i: (0, i, 0))]
        flat = [raw]
    if placed:
        specs = [pl.BlockSpec((groups,) + arrays[0].shape[1:], lambda i: (i, 0, 0, 0))]
    else:
        specs = [pl.BlockSpec((groups,) + arrays[0].shape[1:], lambda i: (i, 0, 0, 0))]
        specs = [pl.BlockSpec(onehot.shape, lambda i: (0, 0, 0))] + specs
        arrays = [onehot] + list(arrays)
    return pl.pallas_call(
        functools.partial(update_kernel, rows, placed, tuple(parts)),
        out_shape=jax.ShapeDtypeStruct((total // SUBLANES, tiles, SUBLANES, LANES), jnp.float32),
        grid=(row_devices // groups,),
        in_specs=[
            pl.BlockSpec(memory_space=pltpu.SMEM),
            pl.BlockSpec((1, cols), lambda i: (0, 0)),
            pl.BlockSpec((rows if not placed else SUBLANES, 1), lambda i: (0 if placed else i, 0)),
            pl.BlockSpec(high.shape, lambda i: (0, 0)),
            pl.BlockSpec(low.shape, lambda i: (0, 0)),
        ]
        + raw_specs
        + specs,
        out_specs=pl.BlockSpec((rows // SUBLANES, tiles, SUBLANES, LANES), lambda i: (i, 0, 0, 0)),
        compiler_params=pltpu.CompilerParams(vmem_limit_bytes=VMEM_LIMIT),
        cost_estimate=LIGHT,
        name="update",
    )(weights, mask, keep, high, low, *flat, *arrays).reshape(-1, LANES)


def finish_kernel(rows, tiles, lane, stride, weighted, has_head, bounds_ref, index_ref, weight_ref, part_hbm, head_ref, base_hbm, out_hbm, held, picked, before, after, part_sem, in_sem, out_sem):
    size = part_hbm.shape[0]
    first, last = bounds_ref[0], bounds_ref[1]
    for source in range(1, bounds_ref.shape[0] // 2):
        first = jnp.minimum(first, bounds_ref[2 * source])
        last = jnp.maximum(last, bounds_ref[2 * source + 1])
    first = first // rows
    steps = last // rows + 1 - first
    lanes = pl.ds(lane, tiles * LANES)

    def block(step):
        return pl.ds(pl.multiple_of((first + step) * rows, rows), rows)

    def fetch(step, slot):
        return pltpu.make_async_copy(out_hbm.at[block(step), lanes], before.at[slot], in_sem.at[slot])

    def store(step, slot):
        return pltpu.make_async_copy(after.at[slot], out_hbm.at[block(step), lanes], out_sem.at[slot])

    part_copy = pltpu.make_async_copy(part_hbm, held.at[pl.ds(0, size)], part_sem)
    part_copy.start()
    fetch(0, 0).start()
    held[pl.ds(size, held.shape[0] - size), :] = jnp.zeros((held.shape[0] - size, LANES), jnp.float32)
    part_copy.wait()

    def body(step, carry):
        slot = lax.rem(step, 2)

        @pl.when(step + 1 < steps)
        def _():
            fetch(step + 1, 1 - slot).start()

        copy_rows(index_ref, (first + step) * rows, held, picked, rows, tiles, stride)
        fetch(step, slot).wait()

        @pl.when(step >= 2)
        def _():
            store(step - 2, slot).wait()

        added = from_view(picked[...], rows, tiles)
        if weighted:
            added = weight_ref[0] * added
        after[slot] = before[slot] + added
        if has_head:

            @pl.when(step == 0)
            def _():
                count = head_ref.shape[0]
                after[0, :count] = after[0, :count] + head_ref[...]

        store(step, slot).start()
        return carry

    lax.fori_loop(0, steps, body, 0)

    @pl.when(steps >= 2)
    def _():
        store(steps - 2, lax.rem(steps, 2)).wait()

    store(steps - 1, lax.rem(steps + 1, 2)).wait()


def finish_part(base, part, bounds, local, count, weights, head, width, has_head):
    total, cols = base.shape
    tiles = cols // LANES
    rows = head.shape[0]
    while rows < 512 and total % (2 * rows) == 0:
        rows *= 2
    lane, stride = 0, SUBLANES
    index = view_base(local, tiles)
    if width:
        tiles -= 1
        lane, stride = LANES, width
        index = local // width * (width * tiles) + local % width
    index = jnp.where((local >= 0) & (local < count), index, part.shape[0])
    spare = -(-(stride * (tiles - 1) + 1) // SUBLANES) * SUBLANES
    return pl.pallas_call(
        functools.partial(finish_kernel, rows, tiles, lane, stride, bool(width), has_head),
        out_shape=jax.ShapeDtypeStruct((total, cols), jnp.float32),
        in_specs=[
            pl.BlockSpec(memory_space=pltpu.SMEM),
            pl.BlockSpec(memory_space=pltpu.SMEM),
            pl.BlockSpec(memory_space=pltpu.SMEM),
            pl.BlockSpec(memory_space=pl.ANY),
            pl.BlockSpec(memory_space=pltpu.VMEM),
            pl.BlockSpec(memory_space=pl.ANY),
        ],
        out_specs=pl.BlockSpec(memory_space=pl.ANY),
        scratch_shapes=[
            pltpu.VMEM((part.shape[0] + spare, LANES), jnp.float32),
            pltpu.VMEM((rows * tiles, LANES), jnp.float32),
            pltpu.VMEM((2, rows, tiles * LANES), jnp.float32),
            pltpu.VMEM((2, rows, tiles * LANES), jnp.float32),
            pltpu.SemaphoreType.DMA,
            pltpu.SemaphoreType.DMA((2,)),
            pltpu.SemaphoreType.DMA((2,)),
        ],
        input_output_aliases={5: 0},
        compiler_params=pltpu.CompilerParams(vmem_limit_bytes=VMEM_LIMIT),
        cost_estimate=LIGHT,
        name="finish",
    )(bounds, index, weights, part, head, base)


def precise(left, right):
    return jnp.dot(left, right, precision=lax.Precision.HIGHEST)


def cholesky_inverse(blocks, pause):
    count = len(blocks)
    size = blocks[0][0].shape[0]
    identity = jnp.eye(size, dtype=jnp.float32)
    factor, inverse = {}, {}
    for b in range(count):
        pivot = jnp.tril(blocks[b][b]) + jnp.tril(blocks[b][b], -1).T
        if b:
            left = jnp.concatenate([factor[b, k] for k in range(b)], axis=1)
            pivot = pivot - precise(left, left.T)
        factor[b, b] = jnp.linalg.cholesky(pivot, symmetrize_input=False)
        inverse[b, b] = jax.scipy.linalg.solve_triangular(factor[b, b], identity, lower=True)
        if b + 1 < count:
            below = jnp.concatenate([blocks[i][b] for i in range(b + 1, count)], axis=0)
            if b:
                rows = [
                    jnp.concatenate([factor[i, k] for k in range(b)], axis=1)
                    for i in range(b + 1, count)
                ]
                below = below - precise(jnp.concatenate(rows, axis=0), left.T)
            below = pause(b, precise(below, inverse[b, b].T))
            for i in range(b + 1, count):
                factor[i, b] = below[(i - b - 1) * size : (i - b) * size]
    zero = jnp.zeros((size, size), jnp.float32)
    for b in range(1, count):
        left = jnp.concatenate([factor[b, k] for k in range(b)], axis=1)
        above = [
            jnp.concatenate([inverse[k, j] if k >= j else zero for j in range(b)], axis=1)
            for k in range(b)
        ]
        solved = -precise(inverse[b, b], precise(left, jnp.concatenate(above, axis=0)))
        for j in range(b):
            inverse[b, j] = solved[:, j * size : (j + 1) * size]
    whole = [
        [
            jnp.concatenate([part[i, j] if i >= j else zero for j in range(count)], axis=1)
            for i in range(count)
        ]
        for part in (factor, inverse)
    ]
    return jnp.concatenate(whole[0], axis=0), jnp.concatenate(whole[1], axis=0)


def shards(
    grace_slab, goce_slab, grace_weight, goce_weight, kaula_prior, row_target, column_target
):
    row_devices = lax.axis_size("prow")
    col_devices = lax.axis_size("pcol")
    row_id = lax.axis_index("prow")
    col_id = lax.axis_index("pcol")
    rows_here, cols_here = grace_slab.shape
    tiles = cols_here // LANES
    row_group = rows_here // row_devices
    col_group = cols_here // col_devices
    per_device = SLAB // (BLOCK * row_devices)
    lead = per_device * BLOCK
    widths = chunk_widths(row_group, lead)
    starts = [sum(widths[:n]) for n in range(len(widths))]
    counts = [row_devices * width for width in widths]
    weights = jnp.concatenate([grace_weight, goce_weight])
    tie = lax.optimization_barrier

    bits = (rows_here - 1).bit_length()
    mask = (1 << bits) - 1
    local = jnp.arange(rows_here, dtype=jnp.int32)
    mine = lax.dynamic_slice_in_dim(row_target, row_id * rows_here, rows_here)
    sources = (jnp.sort(mine * (1 << bits) + local) & mask).reshape(row_devices, row_group)
    source_bases = view_base(sources, tiles)
    chunk_bases = [
        source_bases[:, start : start + width].reshape(-1) for start, width in zip(starts, widths)
    ]
    my_cols = lax.dynamic_slice_in_dim(column_target, col_id * cols_here, cols_here)
    col_ranks = jnp.sum((my_cols[None, :] < my_cols[:, None]).astype(jnp.int32), axis=1)
    distance = jnp.arange(col_devices, dtype=jnp.int32)
    group_iota = jnp.arange(col_group, dtype=jnp.int32)

    def column_onehot(owners):
        return (
            ((col_ranks // col_group)[None, :, None] == owners[:, None, None])
            & ((col_ranks % col_group)[None, :, None] == group_iota[None, None, :])
        ).astype(jnp.bfloat16)

    whole_onehot = column_onehot(distance)
    send_onehot = column_onehot(distance ^ col_id)

    def exchange(packet, axes, devices):
        sent = packet.reshape(devices, -1, packet.shape[-1])
        got = lax.all_to_all(sent, axes, split_axis=0, concat_axis=0, tiled=True)
        return got.reshape(packet.shape)

    def over_rows(packet):
        return exchange(packet, "prow", row_devices)

    def over_cols(pieces):
        got = [pieces[0]]
        for d in range(1, col_devices):
            pairs = [(i, i ^ d) for i in range(col_devices)]
            got.append(lax.ppermute(pieces[d], "pcol", pairs))
        return got

    view = row_view(grace_slab)
    (packet,) = pack(view, chunk_bases[0], whole_onehot, row_devices, widths[0], False)
    first_got = exchange(packet, ("prow", "pcol"), row_devices * col_devices)
    (chunk_bases[1], packet) = tie((chunk_bases[1], packet))
    second = over_cols(pack(view, chunk_bases[1], send_onehot, row_devices, widths[1], True))
    third = pack(view, chunk_bases[2], send_onehot, row_devices, widths[2], True)

    sorted_rows = jnp.sort(row_target.reshape(row_devices, rows_here), axis=1)
    places = lax.dynamic_slice_in_dim(sorted_rows, row_id * row_group, row_group, axis=1)
    places = places - row_id * rows_here
    chunk_places = [
        places[:, start : start + width].reshape(-1) for start, width in zip(starts, widths)
    ]
    ends = [
        jnp.stack([places[:, start], places[:, start + width - 1]], axis=-1).reshape(-1)
        for start, width in zip(starts, widths)
    ]
    positions = jnp.sort(jnp.concatenate(chunk_places) * (1 << bits) + local) & mask
    sorted_cols = jnp.sort(column_target.reshape(col_devices, cols_here), axis=1)
    col_targets = lax.dynamic_slice_in_dim(sorted_cols, col_id * col_group, col_group, axis=1)
    col_targets = col_targets - col_id * cols_here
    col_iota = jnp.arange(cols_here, dtype=jnp.int32)
    take_whole = (col_targets[:, :, None] == col_iota[None, None, :]).astype(jnp.bfloat16)
    take_onehot = jnp.take(take_whole, distance ^ col_id, axis=0)
    order_cols = order_index(cols_here, col_id, col_devices, BLOCK)
    in_panel = order_cols < PANEL
    outside = jnp.where(in_panel, 0.0, 1.0)[None, :].astype(jnp.float32)
    out = goce_slab * (goce_weight[0] * outside)

    added = [goce_rows(where, weights, goce_slab, row_devices) for where in chunk_places]

    second, third, added, ends, positions, take_onehot, take_whole, out = tie(
        (second, third, added, ends, positions, take_onehot, take_whole, out)
    )
    third = over_cols(third)
    (second_packet,) = mix(second, take_onehot, (tiles,))
    second_packet, first_got = tie((second_packet, first_got))
    second_got = over_rows(second_packet)
    panels = [panel_part(first_got, added[0], weights, take_whole[:, :, :BLOCK])]
    panel_blocks = PANEL // BLOCK
    my_lead = jnp.take(panels[0], positions[:lead], axis=0).reshape(per_device, BLOCK, BLOCK)
    lead_order = jnp.arange(per_device, dtype=jnp.int32) * row_devices + row_id
    my_diag = jnp.where(lead_order[:, None] == col_id, kaula_prior[None, :BLOCK], 0.0)
    my_lead = my_lead + my_diag[:, :, None] * jnp.eye(BLOCK, dtype=jnp.float32)
    lead_cols = lax.all_gather(my_lead, "prow", axis=0)
    lead_cols = lead_cols.transpose(1, 0, 2, 3).reshape(-1, BLOCK, BLOCK)
    outer = [n for n in range(tiles) if (n + 1) * col_devices > panel_blocks]
    lead_parts = []
    for d in range(col_devices):
        wanted = jnp.array(outer, dtype=jnp.int32) * col_devices + (col_id ^ d)
        lead_parts.append(
            jnp.concatenate([lead_cols[:panel_blocks], jnp.take(lead_cols, wanted, axis=0)], axis=0)
        )
    lead_all = jnp.take(jnp.stack(over_cols(lead_parts)), distance ^ col_id, axis=0)[:panel_blocks]

    third_packets = list(mix(third, take_onehot, (1, tiles - 1)))
    lead_all, third_packets = tie((lead_all, third_packets))
    blocks = [[lead_all[j, i] for j in range(i + 1)] for i in range(panel_blocks)]
    late = {}

    def pause(step, value):
        if step == 0:
            value, late["second"], packet = tie((value, second_got, third_packets[0]))
            late["panel"] = over_rows(packet)
        if step == panel_blocks - 2:
            value, late["panel"], packet = tie((value, late["panel"], third_packets[1]))
            late["rest"] = over_rows(packet)
        return value

    factor, inverse = cholesky_inverse(blocks, pause)
    second_got, third_panel, third_rest = late["second"], late["panel"], late["rest"]
    col_rows = []
    for n in range(tiles):
        if n in outer:
            rows = lead_all[:, panel_blocks + outer.index(n)]
            col_rows.append(rows.transpose(1, 0, 2).reshape(BLOCK, PANEL))
        else:
            col_rows.append(jnp.zeros((BLOCK, PANEL), jnp.float32))
    col_rows = jnp.concatenate(col_rows, axis=0)
    solved = precise(inverse, col_rows.T)
    panel_iota = jnp.arange(PANEL, dtype=jnp.int32)
    identity = (panel_iota[:, None] == order_cols[None, :]).astype(jnp.float32)
    matrix = precise(inverse.T, jnp.where(in_panel[None, :], identity, -solved))
    matrix_high, matrix_low = split_array(matrix)

    order_rows = order_index(lead, row_id, row_devices, BLOCK)
    on_diagonal = order_rows[:, None] == order_cols[None, :]
    known = jnp.take(
        jnp.take(factor, jnp.minimum(order_rows, PANEL - 1), axis=0),
        jnp.minimum(order_cols, PANEL - 1),
        axis=1,
    )
    in_block = (order_rows[:, None] < PANEL) & in_panel[None, :]
    head = jnp.where(in_block, known, jnp.where(on_diagonal, kaula_prior[None, :], 0.0))
    first = chunk_places[0]
    first_order = (first // BLOCK * row_devices + row_id) * BLOCK + first % BLOCK
    keep = jnp.where(first_order < PANEL, 0.0, 1.0)[:, None].astype(jnp.float32)

    panels[0], third = tie((panels[0], third))
    for n, got in ((1, second_got), (2, third_panel)):
        panels.append(grace_weight[0] * got[:, 0].reshape(-1, BLOCK) + added[n])
    raws = [lax.all_gather(panel, "pcol", axis=0) for panel in panels]
    arrays = [[first_got], [second_got], [third_panel]]
    offset = 0
    for n in range(len(widths)):
        part = update_part(
            arrays[n],
            raws[n],
            keep,
            weights,
            outside,
            take_whole if n == 0 else None,
            matrix_high,
            matrix_low,
        )
        out = finish_part(
            out, part, ends[n], positions - offset, counts[n], weights, head, 0, n == 0
        )
        offset += counts[n]
    out, third_rest = tie((out, third_rest))
    return finish_part(
        out,
        third_rest.reshape(-1, LANES),
        ends[-1],
        positions - (offset - counts[-1]),
        counts[-1],
        weights,
        head,
        widths[-1],
        False,
    )


def solution(mesh):
    return jax.shard_map(
        shards,
        mesh=mesh,
        in_specs=(P("prow", "pcol"), P("prow", "pcol"), P(), P(), P("pcol"), P(), P()),
        out_specs=P("prow", "pcol"),
        check_vma=False,
    )
```

```python
import functools

import jax
import jax.numpy as jnp
from jax import lax
from jax.experimental import pallas as pl
from jax.experimental.pallas import tpu as pltpu
from jax.sharding import PartitionSpec as P

SLAB = 2048
PANEL = 512
BLOCK = 128
LANES = 128
SUBLANES = 8
REST_STEP = 1
LIGHT = pl.CostEstimate(flops=1, bytes_accessed=1, transcendentals=0)
HEAVY = pl.CostEstimate(flops=1, bytes_accessed=700_000_000, transcendentals=0)
VMEM_LIMIT = 56 * 1024 * 1024


def order_index(amount, device, groups, block_size):
    local = jnp.arange(amount, dtype=jnp.int32)
    return (local // block_size * groups + device) * block_size + local % block_size


def group_step(groups, width, most=1024):
    best = 1
    for size in range(1, groups + 1):
        if groups % size == 0 and size * width <= most:
            best = size
    return best


def chunk_widths(total, head):
    first = max(head, total * 7 // 22 // 16 * 16)
    second = min(total - first, total * 25 // 88) // 16 * 16
    return first, second, total - first - second


def row_view(array):
    rows, cols = array.shape
    tiles = cols // LANES
    shaped = array.reshape(rows // SUBLANES, SUBLANES, tiles, LANES)
    return shaped.transpose(0, 2, 1, 3).reshape(rows * tiles, LANES)


def view_base(index, tiles):
    return index // SUBLANES * (SUBLANES * tiles) + index % SUBLANES


def split(value):
    high = value.astype(jnp.bfloat16)
    low = (value - high.astype(jnp.float32)).astype(jnp.bfloat16)
    return high, low


def split_array(value):
    high = lax.reduce_precision(value, 8, 7)
    return high.astype(jnp.bfloat16), (value - high).astype(jnp.bfloat16)


def product(left, right):
    return jnp.dot(left, right, preferred_element_type=jnp.float32)


def copy_rows(index_ref, first, source, target, count, tiles, stride):
    def move(step, carry):
        for lane in range(SUBLANES):
            base = index_ref[first + step * SUBLANES + lane]
            target[pl.ds(step * SUBLANES * tiles + lane, tiles, stride=SUBLANES), :] = source[
                pl.ds(base, tiles, stride=stride), :
            ]
        return carry

    lax.fori_loop(0, count // SUBLANES, move, 0, unroll=4)


def from_view(value, rows, tiles):
    shaped = value.reshape(rows // SUBLANES, tiles, SUBLANES, LANES)
    return jnp.concatenate([shaped[:, t].reshape(rows, LANES) for t in range(tiles)], axis=1)


def pack_kernel(rows, tiles, index_ref, source_hbm, onehot_ref, *refs):
    outs, (held, picked, sem) = refs[:-3], refs[-3:]
    step = pl.program_id(0)

    @pl.when(step == 0)
    def _():
        copy = pltpu.make_async_copy(source_hbm, held, sem)
        copy.start()
        copy.wait()

    copy_rows(index_ref, step * rows, held, picked, rows, tiles, SUBLANES)
    high, low = split(from_view(picked[...], rows, tiles))
    places = [(out, None) for out in outs]
    if len(outs) == 1:
        places = [(outs[0], d) for d in range(outs[0].shape[1])]
    lanes = onehot_ref.shape[2]
    if lanes % LANES == 0:
        whole = jnp.concatenate([onehot_ref[d] for d in range(len(places))], axis=1)
        moved = product(high, whole) + product(low, whole)
        parts = [moved[:, d * lanes : (d + 1) * lanes] for d in range(len(places))]
    else:
        parts = [
            product(high, onehot_ref[d]) + product(low, onehot_ref[d]) for d in range(len(places))
        ]
    for part, (out, d) in zip(parts, places):
        if d is None:
            out[...] = part.reshape(out.shape)
        else:
            out[:, d] = part.reshape(out.shape[0], out.shape[2], lanes)


def pack(view, bases, onehot, row_devices, width, apart):
    col_devices, cols, group = onehot.shape
    tiles = cols // LANES
    groups = group_step(row_devices, width)
    rows = groups * width
    if apart:
        shapes = [jax.ShapeDtypeStruct((row_devices, width, group), jnp.float32)] * col_devices
        specs = [pl.BlockSpec((groups, width, group), lambda i: (i, 0, 0))] * col_devices
    else:
        shapes = [jax.ShapeDtypeStruct((row_devices, col_devices, width, group), jnp.float32)]
        specs = [pl.BlockSpec((groups, col_devices, width, group), lambda i: (i, 0, 0, 0))]
    return pl.pallas_call(
        functools.partial(pack_kernel, rows, tiles),
        out_shape=shapes,
        grid=(row_devices // groups,),
        in_specs=[
            pl.BlockSpec(memory_space=pltpu.SMEM),
            pl.BlockSpec(memory_space=pl.ANY),
            pl.BlockSpec(onehot.shape, lambda i: (0, 0, 0)),
        ],
        out_specs=specs,
        scratch_shapes=[
            pltpu.VMEM(view.shape, jnp.float32),
            pltpu.VMEM((rows * tiles, LANES), jnp.float32),
            pltpu.SemaphoreType.DMA,
        ],
        compiler_params=pltpu.CompilerParams(vmem_limit_bytes=VMEM_LIMIT),
        cost_estimate=LIGHT,
        name="pack",
    )(bases, view, onehot)


def place_columns(pieces, onehot_ref, rows):
    if len(pieces[0].shape) == 4:
        pieces = [pieces[0][:, c] for c in range(pieces[0].shape[1])]
    values = [piece[...].reshape(rows, piece.shape[-1]) for piece in pieces]
    if values[0].shape[1] % LANES == 0:
        high, low = split(jnp.concatenate(values, axis=1))
        whole = onehot_ref[...].reshape(high.shape[1], onehot_ref.shape[2])
        return product(high, whole) + product(low, whole)
    total = None
    for d, value in enumerate(values):
        high, low = split(value)
        part = product(high, onehot_ref[d]) + product(low, onehot_ref[d])
        total = part if total is None else total + part
    return total


def mix_kernel(rows, counts, onehot_ref, *refs):
    pieces, outs = refs[: -len(counts)], refs[-len(counts) :]
    moved = place_columns(pieces, onehot_ref, rows)
    tile = 0
    for count, out in zip(counts, outs):
        for t in range(count):
            part = moved[:, (tile + t) * LANES : (tile + t + 1) * LANES]
            out[:, t] = part.reshape(out.shape[0], out.shape[2], LANES)
        tile += count


def mix(pieces, onehot, counts):
    row_devices, width, lanes = pieces[0].shape
    groups = group_step(row_devices, width)
    rows = groups * width
    return pl.pallas_call(
        functools.partial(mix_kernel, rows, counts),
        out_shape=[
            jax.ShapeDtypeStruct((row_devices, count, width, LANES), jnp.float32) for count in counts
        ],
        grid=(row_devices // groups,),
        in_specs=[pl.BlockSpec(onehot.shape, lambda i: (0, 0, 0))]
        + [pl.BlockSpec((groups, width, lanes), lambda i: (i, 0, 0))] * len(pieces),
        out_specs=[
            pl.BlockSpec((groups, count, width, LANES), lambda i: (i, 0, 0, 0)) for count in counts
        ],
        compiler_params=pltpu.CompilerParams(vmem_limit_bytes=VMEM_LIMIT),
        cost_estimate=LIGHT,
        name="mix",
    )(onehot, *pieces)


def goce_rows_kernel(rows, index_ref, weight_ref, goce_hbm, out_ref, held, picked, sem):
    step = pl.program_id(0)

    @pl.when(step == 0)
    def _():
        copy = pltpu.make_async_copy(goce_hbm.at[:, pl.ds(0, BLOCK)], held, sem)
        copy.start()
        copy.wait()

    copy_rows(index_ref, step * rows, held, picked, rows, 1, 1)
    out_ref[...] = weight_ref[1] * picked[...]


def goce_rows(places, weights, goce, row_devices):
    total = places.shape[0]
    rows = total // row_devices * group_step(row_devices, total // row_devices)
    return pl.pallas_call(
        functools.partial(goce_rows_kernel, rows),
        out_shape=jax.ShapeDtypeStruct((total, BLOCK), jnp.float32),
        grid=(total // rows,),
        in_specs=[
            pl.BlockSpec(memory_space=pltpu.SMEM),
            pl.BlockSpec(memory_space=pltpu.SMEM),
            pl.BlockSpec(memory_space=pl.ANY),
        ],
        out_specs=pl.BlockSpec((rows, BLOCK), lambda i: (i, 0)),
        scratch_shapes=[
            pltpu.VMEM((goce.shape[0], BLOCK), jnp.float32),
            pltpu.VMEM((rows, BLOCK), jnp.float32),
            pltpu.SemaphoreType.DMA,
        ],
        compiler_params=pltpu.CompilerParams(vmem_limit_bytes=VMEM_LIMIT),
        cost_estimate=LIGHT,
        name="goce_rows",
    )(places, weights, goce)


def panel_kernel(rows, weight_ref, added_ref, onehot_ref, received_ref, out_ref):
    moved = place_columns([received_ref], onehot_ref, rows)
    out_ref[...] = weight_ref[0] * moved + added_ref[...]


def panel_part(received, added, weights, onehot):
    row_devices, width = received.shape[0], received.shape[2]
    groups = group_step(row_devices, width)
    rows = groups * width
    return pl.pallas_call(
        functools.partial(panel_kernel, rows),
        out_shape=jax.ShapeDtypeStruct((row_devices * width, BLOCK), jnp.float32),
        grid=(row_devices // groups,),
        in_specs=[
            pl.BlockSpec(memory_space=pltpu.SMEM),
            pl.BlockSpec((rows, BLOCK), lambda i: (i, 0)),
            pl.BlockSpec(onehot.shape, lambda i: (0, 0, 0)),
            pl.BlockSpec((groups,) + received.shape[1:], lambda i: (i, 0, 0, 0)),
        ],
        out_specs=pl.BlockSpec((rows, BLOCK), lambda i: (i, 0)),
        compiler_params=pltpu.CompilerParams(vmem_limit_bytes=VMEM_LIMIT),
        cost_estimate=HEAVY,
        name="panel",
    )(weights, added, onehot, received)


def update_kernel(rows, placed, parts, weight_ref, mask_ref, keep_ref, high_ref, low_ref, *refs):
    step = pl.program_id(0)
    raw_count = sum(count for _, _, count in parts)
    raws, arrays, out_ref = refs[:raw_count], refs[raw_count:-1], refs[-1]

    def compute(pieces):
        raw = jnp.concatenate(pieces, axis=1)
        if not placed:
            raw = raw * keep_ref[...]
        high, low = split(raw)
        total = product(high, high_ref[...]) + product(low, high_ref[...])
        total = total + product(high, low_ref[...])
        if placed:
            shape = arrays[0].shape
            tiles = [arrays[0][:, t].reshape(rows, LANES) for t in range(shape[1])]
        else:
            moved = place_columns(arrays[1:], arrays[0], rows)
            tiles = [moved[:, t * LANES : (t + 1) * LANES] for t in range(moved.shape[1] // LANES)]
        for t in range(total.shape[1] // LANES):
            lanes = slice(t * LANES, (t + 1) * LANES)
            part = total[:, lanes]
            if t < len(tiles):
                part = part + (weight_ref[0] * mask_ref[:, lanes]) * tiles[t]
            out_ref[:, t] = part.reshape(rows // SUBLANES, SUBLANES, LANES)

    used = 0
    for first, steps, count in parts:
        mine = raws[used : used + count]
        used += count

        @pl.when((step >= first) & (step < first + steps))
        def _():
            if count == 1:
                compute([mine[0][p] for p in range(high_ref.shape[0] // BLOCK)])
            else:
                compute([ref[...] for ref in mine])


def part_map(first, steps, step):
    return (jnp.clip(step - first, 0, steps - 1), 0)


def update_part(arrays, raw, keep, weights, mask, onehot, high, low):
    placed = onehot is None
    row_devices, width, lanes = arrays[0].shape[0], arrays[0].shape[-2], arrays[0].shape[-1]
    cols = high.shape[1]
    tiles = cols // LANES
    groups = group_step(row_devices, width)
    rows = groups * width
    total = row_devices * width
    if isinstance(raw, list):
        parts, raw_specs, flat, first = [], [], [], 0
        for pieces in raw:
            steps = pieces[0].shape[0] // rows
            parts.append((first, steps, len(pieces)))
            place = functools.partial(part_map, first, steps)
            raw_specs += [pl.BlockSpec((rows, BLOCK), place)] * len(pieces)
            flat += pieces
            first += steps
    else:
        parts = [(0, row_devices // groups, 1)]
        raw_specs = [pl.BlockSpec((high.shape[0] // BLOCK, rows, BLOCK), lambda i: (0, i, 0))]
        flat = [raw]
    if placed:
        specs = [pl.BlockSpec((groups,) + arrays[0].shape[1:], lambda i: (i, 0, 0, 0))]
    else:
        specs = [pl.BlockSpec((groups,) + arrays[0].shape[1:], lambda i: (i, 0, 0, 0))]
        specs = [pl.BlockSpec(onehot.shape, lambda i: (0, 0, 0))] + specs
        arrays = [onehot] + list(arrays)
    return pl.pallas_call(
        functools.partial(update_kernel, rows, placed, tuple(parts)),
        out_shape=jax.ShapeDtypeStruct((total // SUBLANES, tiles, SUBLANES, LANES), jnp.float32),
        grid=(row_devices // groups,),
        in_specs=[
            pl.BlockSpec(memory_space=pltpu.SMEM),
            pl.BlockSpec((1, cols), lambda i: (0, 0)),
            pl.BlockSpec((rows if not placed else SUBLANES, 1), lambda i: (0 if placed else i, 0)),
            pl.BlockSpec(high.shape, lambda i: (0, 0)),
            pl.BlockSpec(low.shape, lambda i: (0, 0)),
        ]
        + raw_specs
        + specs,
        out_specs=pl.BlockSpec((rows // SUBLANES, tiles, SUBLANES, LANES), lambda i: (i, 0, 0, 0)),
        compiler_params=pltpu.CompilerParams(vmem_limit_bytes=VMEM_LIMIT),
        cost_estimate=LIGHT,
        name="update",
    )(weights, mask, keep, high, low, *flat, *arrays).reshape(-1, LANES)


def finish_kernel(rows, tiles, lane, stride, weighted, has_head, bounds_ref, index_ref, weight_ref, part_hbm, head_ref, base_hbm, out_hbm, held, picked, before, after, part_sem, in_sem, out_sem):
    size = part_hbm.shape[0]
    first, last = bounds_ref[0], bounds_ref[1]
    for source in range(1, bounds_ref.shape[0] // 2):
        first = jnp.minimum(first, bounds_ref[2 * source])
        last = jnp.maximum(last, bounds_ref[2 * source + 1])
    first = first // rows
    steps = last // rows + 1 - first
    lanes = pl.ds(lane, tiles * LANES)

    def block(step):
        return pl.ds(pl.multiple_of((first + step) * rows, rows), rows)

    def fetch(step, slot):
        return pltpu.make_async_copy(out_hbm.at[block(step), lanes], before.at[slot], in_sem.at[slot])

    def store(step, slot):
        return pltpu.make_async_copy(after.at[slot], out_hbm.at[block(step), lanes], out_sem.at[slot])

    part_copy = pltpu.make_async_copy(part_hbm, held.at[pl.ds(0, size)], part_sem)
    part_copy.start()
    fetch(0, 0).start()
    held[pl.ds(size, held.shape[0] - size), :] = jnp.zeros((held.shape[0] - size, LANES), jnp.float32)
    part_copy.wait()

    def body(step, carry):
        slot = lax.rem(step, 2)

        @pl.when(step + 1 < steps)
        def _():
            fetch(step + 1, 1 - slot).start()

        copy_rows(index_ref, (first + step) * rows, held, picked, rows, tiles, stride)
        fetch(step, slot).wait()

        @pl.when(step >= 2)
        def _():
            store(step - 2, slot).wait()

        added = from_view(picked[...], rows, tiles)
        if weighted:
            added = weight_ref[0] * added
        after[slot] = before[slot] + added
        if has_head:

            @pl.when(step == 0)
            def _():
                count = head_ref.shape[0]
                after[0, :count] = after[0, :count] + head_ref[...]

        store(step, slot).start()
        return carry

    lax.fori_loop(0, steps, body, 0)

    @pl.when(steps >= 2)
    def _():
        store(steps - 2, lax.rem(steps, 2)).wait()

    store(steps - 1, lax.rem(steps + 1, 2)).wait()


def finish_index(local, count, tiles, width):
    index, size = view_base(local, tiles), count * tiles
    if width:
        index = local // width * (width * (tiles - 1)) + local % width
        size = count * (tiles - 1)
    return jnp.where((local >= 0) & (local < count), index, size)


def finish_part(base, part, bounds, index, weights, head, width, has_head):
    total, cols = base.shape
    tiles = cols // LANES
    rows = head.shape[0]
    while rows < 512 and total % (2 * rows) == 0:
        rows *= 2
    lane, stride = 0, SUBLANES
    if width:
        tiles -= 1
        lane, stride = LANES, width
    spare = -(-(stride * (tiles - 1) + 1) // SUBLANES) * SUBLANES
    return pl.pallas_call(
        functools.partial(finish_kernel, rows, tiles, lane, stride, bool(width), has_head),
        out_shape=jax.ShapeDtypeStruct((total, cols), jnp.float32),
        in_specs=[
            pl.BlockSpec(memory_space=pltpu.SMEM),
            pl.BlockSpec(memory_space=pltpu.SMEM),
            pl.BlockSpec(memory_space=pltpu.SMEM),
            pl.BlockSpec(memory_space=pl.ANY),
            pl.BlockSpec(memory_space=pltpu.VMEM),
            pl.BlockSpec(memory_space=pl.ANY),
        ],
        out_specs=pl.BlockSpec(memory_space=pl.ANY),
        scratch_shapes=[
            pltpu.VMEM((part.shape[0] + spare, LANES), jnp.float32),
            pltpu.VMEM((rows * tiles, LANES), jnp.float32),
            pltpu.VMEM((2, rows, tiles * LANES), jnp.float32),
            pltpu.VMEM((2, rows, tiles * LANES), jnp.float32),
            pltpu.SemaphoreType.DMA,
            pltpu.SemaphoreType.DMA((2,)),
            pltpu.SemaphoreType.DMA((2,)),
        ],
        input_output_aliases={5: 0},
        compiler_params=pltpu.CompilerParams(vmem_limit_bytes=VMEM_LIMIT),
        cost_estimate=LIGHT,
        name="finish",
    )(bounds, index, weights, part, head, base)


def precise(left, right):
    return jnp.dot(left, right, precision=lax.Precision.HIGHEST)


def cholesky_inverse(blocks, pause):
    count = len(blocks)
    size = blocks[0][0].shape[0]
    identity = jnp.eye(size, dtype=jnp.float32)
    factor, inverse = {}, {}
    for b in range(count):
        pivot = jnp.tril(blocks[b][b]) + jnp.tril(blocks[b][b], -1).T
        if b:
            left = jnp.concatenate([factor[b, k] for k in range(b)], axis=1)
            pivot = pivot - precise(left, left.T)
        factor[b, b] = jnp.linalg.cholesky(pivot, symmetrize_input=False)
        inverse[b, b] = jax.scipy.linalg.solve_triangular(factor[b, b], identity, lower=True)
        if b + 1 < count:
            below = jnp.concatenate([blocks[i][b] for i in range(b + 1, count)], axis=0)
            if b:
                rows = [
                    jnp.concatenate([factor[i, k] for k in range(b)], axis=1)
                    for i in range(b + 1, count)
                ]
                below = below - precise(jnp.concatenate(rows, axis=0), left.T)
            below = pause(b, precise(below, inverse[b, b].T))
            for i in range(b + 1, count):
                factor[i, b] = below[(i - b - 1) * size : (i - b) * size]
    zero = jnp.zeros((size, size), jnp.float32)
    for b in range(1, count):
        left = jnp.concatenate([factor[b, k] for k in range(b)], axis=1)
        above = [
            jnp.concatenate([inverse[k, j] if k >= j else zero for j in range(b)], axis=1)
            for k in range(b)
        ]
        solved = -precise(inverse[b, b], precise(left, jnp.concatenate(above, axis=0)))
        for j in range(b):
            inverse[b, j] = solved[:, j * size : (j + 1) * size]
    whole = [
        [
            jnp.concatenate([part[i, j] if i >= j else zero for j in range(count)], axis=1)
            for i in range(count)
        ]
        for part in (factor, inverse)
    ]
    return jnp.concatenate(whole[0], axis=0), jnp.concatenate(whole[1], axis=0)


def shards(
    grace_slab, goce_slab, grace_weight, goce_weight, kaula_prior, row_target, column_target
):
    row_devices = lax.axis_size("prow")
    col_devices = lax.axis_size("pcol")
    row_id = lax.axis_index("prow")
    col_id = lax.axis_index("pcol")
    rows_here, cols_here = grace_slab.shape
    tiles = cols_here // LANES
    row_group = rows_here // row_devices
    col_group = cols_here // col_devices
    per_device = SLAB // (BLOCK * row_devices)
    lead = per_device * BLOCK
    widths = chunk_widths(row_group, lead)
    starts = [sum(widths[:n]) for n in range(len(widths))]
    counts = [row_devices * width for width in widths]
    weights = jnp.concatenate([grace_weight, goce_weight])
    tie = lax.optimization_barrier

    bits = (rows_here - 1).bit_length()
    mask = (1 << bits) - 1
    local = jnp.arange(rows_here, dtype=jnp.int32)
    mine = lax.dynamic_slice_in_dim(row_target, row_id * rows_here, rows_here)
    sources = (jnp.sort(mine * (1 << bits) + local) & mask).reshape(row_devices, row_group)
    source_bases = view_base(sources, tiles)
    chunk_bases = [
        source_bases[:, start : start + width].reshape(-1) for start, width in zip(starts, widths)
    ]
    my_cols = lax.dynamic_slice_in_dim(column_target, col_id * cols_here, cols_here)
    col_ranks = jnp.sum((my_cols[None, :] < my_cols[:, None]).astype(jnp.int32), axis=1)
    distance = jnp.arange(col_devices, dtype=jnp.int32)
    group_iota = jnp.arange(col_group, dtype=jnp.int32)

    def column_onehot(owners):
        return (
            ((col_ranks // col_group)[None, :, None] == owners[:, None, None])
            & ((col_ranks % col_group)[None, :, None] == group_iota[None, None, :])
        ).astype(jnp.bfloat16)

    whole_onehot = column_onehot(distance)
    send_onehot = column_onehot(distance ^ col_id)

    def exchange(packet, axes, devices):
        sent = packet.reshape(devices, -1, packet.shape[-1])
        got = lax.all_to_all(sent, axes, split_axis=0, concat_axis=0, tiled=True)
        return got.reshape(packet.shape)

    def over_rows(packet):
        return exchange(packet, "prow", row_devices)

    def over_cols(pieces):
        got = [pieces[0]]
        for d in range(1, col_devices):
            pairs = [(i, i ^ d) for i in range(col_devices)]
            got.append(lax.ppermute(pieces[d], "pcol", pairs))
        return got

    view = row_view(grace_slab)
    (packet,) = pack(view, chunk_bases[0], whole_onehot, row_devices, widths[0], False)
    first_got = exchange(packet, ("prow", "pcol"), row_devices * col_devices)
    (chunk_bases[1], packet) = tie((chunk_bases[1], packet))
    second = over_cols(pack(view, chunk_bases[1], send_onehot, row_devices, widths[1], True))
    third = pack(view, chunk_bases[2], send_onehot, row_devices, widths[2], True)

    sorted_rows = jnp.sort(row_target.reshape(row_devices, rows_here), axis=1)
    places = lax.dynamic_slice_in_dim(sorted_rows, row_id * row_group, row_group, axis=1)
    places = places - row_id * rows_here
    chunk_places = [
        places[:, start : start + width].reshape(-1) for start, width in zip(starts, widths)
    ]
    ends = [
        jnp.stack([places[:, start], places[:, start + width - 1]], axis=-1).reshape(-1)
        for start, width in zip(starts, widths)
    ]
    positions = jnp.sort(jnp.concatenate(chunk_places) * (1 << bits) + local) & mask
    sorted_cols = jnp.sort(column_target.reshape(col_devices, cols_here), axis=1)
    col_targets = lax.dynamic_slice_in_dim(sorted_cols, col_id * col_group, col_group, axis=1)
    col_targets = col_targets - col_id * cols_here
    col_iota = jnp.arange(cols_here, dtype=jnp.int32)
    take_whole = (col_targets[:, :, None] == col_iota[None, None, :]).astype(jnp.bfloat16)
    take_onehot = jnp.take(take_whole, distance ^ col_id, axis=0)
    order_cols = order_index(cols_here, col_id, col_devices, BLOCK)
    in_panel = order_cols < PANEL
    outside = jnp.where(in_panel, 0.0, 1.0)[None, :].astype(jnp.float32)
    out = goce_slab * (goce_weight[0] * outside)

    first = chunk_places[0]
    first_order = (first // BLOCK * row_devices + row_id) * BLOCK + first % BLOCK
    keep = jnp.where(first_order < PANEL, 0.0, 1.0)[:, None].astype(jnp.float32)

    offsets = [sum(counts[:n]) for n in range(len(counts))]
    indices = [
        finish_index(positions - offset, count, tiles, 0) for offset, count in zip(offsets, counts)
    ]
    indices.append(finish_index(positions - offsets[-1], counts[-1], tiles, widths[-1]))
    added = [goce_rows(where, weights, goce_slab, row_devices) for where in chunk_places]

    second, third, added, ends, positions, take_onehot, take_whole, out, keep, indices = tie(
        (second, third, added, ends, positions, take_onehot, take_whole, out, keep, indices)
    )
    third = over_cols(third)
    (second_packet,) = mix(second, take_onehot, (tiles,))
    second_packet, first_got = tie((second_packet, first_got))
    second_got = over_rows(second_packet)
    panels = [panel_part(first_got, added[0], weights, take_whole[:, :, :BLOCK])]
    panel_blocks = PANEL // BLOCK
    my_lead = jnp.take(panels[0], positions[:lead], axis=0).reshape(per_device, BLOCK, BLOCK)
    lead_order = jnp.arange(per_device, dtype=jnp.int32) * row_devices + row_id
    my_diag = jnp.where(lead_order[:, None] == col_id, kaula_prior[None, :BLOCK], 0.0)
    my_lead = my_lead + my_diag[:, :, None] * jnp.eye(BLOCK, dtype=jnp.float32)
    lead_cols = lax.all_gather(my_lead, "prow", axis=0)
    lead_cols = lead_cols.transpose(1, 0, 2, 3).reshape(-1, BLOCK, BLOCK)
    outer = [n for n in range(tiles) if (n + 1) * col_devices > panel_blocks]
    lead_parts = []
    for d in range(col_devices):
        wanted = jnp.array(outer, dtype=jnp.int32) * col_devices + (col_id ^ d)
        lead_parts.append(
            jnp.concatenate([lead_cols[:panel_blocks], jnp.take(lead_cols, wanted, axis=0)], axis=0)
        )
    lead_all = jnp.take(jnp.stack(over_cols(lead_parts)), distance ^ col_id, axis=0)[:panel_blocks]

    third_packets = list(mix(third, take_onehot, (1, tiles - 1)))
    lead_all, third_packets = tie((lead_all, third_packets))
    blocks = [[lead_all[j, i] for j in range(i + 1)] for i in range(panel_blocks)]
    late = {}

    def pause(step, value):
        if step == 0:
            value, late["second"], packet = tie((value, second_got, third_packets[0]))
            late["panel"] = over_rows(packet)
        if step == min(REST_STEP, panel_blocks - 2):
            value, late["panel"], packet = tie((value, late["panel"], third_packets[1]))
            late["rest"] = over_rows(packet)
        return value

    factor, inverse = cholesky_inverse(blocks, pause)
    second_got, third_panel, third_rest = late["second"], late["panel"], late["rest"]
    col_rows = []
    for n in range(tiles):
        if n in outer:
            rows = lead_all[:, panel_blocks + outer.index(n)]
            col_rows.append(rows.transpose(1, 0, 2).reshape(BLOCK, PANEL))
        else:
            col_rows.append(jnp.zeros((BLOCK, PANEL), jnp.float32))
    col_rows = jnp.concatenate(col_rows, axis=0)
    solved = precise(inverse, col_rows.T)
    panel_iota = jnp.arange(PANEL, dtype=jnp.int32)
    identity = (panel_iota[:, None] == order_cols[None, :]).astype(jnp.float32)
    matrix = precise(inverse.T, jnp.where(in_panel[None, :], identity, -solved))
    matrix_high, matrix_low = split_array(matrix)

    order_rows = order_index(lead, row_id, row_devices, BLOCK)
    on_diagonal = order_rows[:, None] == order_cols[None, :]
    known = jnp.take(
        jnp.take(factor, jnp.minimum(order_rows, PANEL - 1), axis=0),
        jnp.minimum(order_cols, PANEL - 1),
        axis=1,
    )
    in_block = (order_rows[:, None] < PANEL) & in_panel[None, :]
    head = jnp.where(in_block, known, jnp.where(on_diagonal, kaula_prior[None, :], 0.0))
    panels[0], third = tie((panels[0], third))
    for n, got in ((1, second_got), (2, third_panel)):
        panels.append(grace_weight[0] * got[:, 0].reshape(-1, BLOCK) + added[n])
    raws = [lax.all_gather(panel, "pcol", axis=0) for panel in panels]
    arrays = [[first_got], [second_got], [third_panel]]
    for n in range(len(widths)):
        part = update_part(
            arrays[n],
            raws[n],
            keep,
            weights,
            outside,
            take_whole if n == 0 else None,
            matrix_high,
            matrix_low,
        )
        out = finish_part(out, part, ends[n], indices[n], weights, head, 0, n == 0)
    out, third_rest = tie((out, third_rest))
    rest_rows = third_rest.reshape(-1, LANES)
    return finish_part(out, rest_rows, ends[-1], indices[-1], weights, head, widths[-1], False)


def solution(mesh):
    return jax.shard_map(
        shards,
        mesh=mesh,
        in_specs=(P("prow", "pcol"), P("prow", "pcol"), P(), P(), P("pcol"), P(), P()),
        out_specs=P("prow", "pcol"),
        check_vma=False,
    )
```

```python
import functools

import jax
import jax.numpy as jnp
from jax import lax
from jax.experimental import pallas as pl
from jax.experimental.pallas import tpu as pltpu
from jax.sharding import PartitionSpec as P

SLAB = 2048
PANEL = 512
BLOCK = 128
LANES = 128
SUBLANES = 8
REST_STEP = 2
LIGHT = pl.CostEstimate(flops=1, bytes_accessed=1, transcendentals=0)
HEAVY = pl.CostEstimate(flops=1, bytes_accessed=700_000_000, transcendentals=0)
VMEM_LIMIT = 56 * 1024 * 1024


def order_index(amount, device, groups, block_size):
    local = jnp.arange(amount, dtype=jnp.int32)
    return (local // block_size * groups + device) * block_size + local % block_size


def group_step(groups, width, most=1024):
    best = 1
    for size in range(1, groups + 1):
        if groups % size == 0 and size * width <= most:
            best = size
    return best


def chunk_widths(total, head):
    first = max(head, total * 7 // 22 // 16 * 16)
    second = min(total - first, total * 25 // 88) // 16 * 16
    return first, second, total - first - second


def row_view(array):
    rows, cols = array.shape
    tiles = cols // LANES
    shaped = array.reshape(rows // SUBLANES, SUBLANES, tiles, LANES)
    return shaped.transpose(0, 2, 1, 3).reshape(rows * tiles, LANES)


def view_base(index, tiles):
    return index // SUBLANES * (SUBLANES * tiles) + index % SUBLANES


def split(value):
    high = value.astype(jnp.bfloat16)
    low = (value - high.astype(jnp.float32)).astype(jnp.bfloat16)
    return high, low


def split_array(value):
    high = lax.reduce_precision(value, 8, 7)
    return high.astype(jnp.bfloat16), (value - high).astype(jnp.bfloat16)


def product(left, right):
    return jnp.dot(left, right, preferred_element_type=jnp.float32)


def copy_rows(index_ref, first, source, target, count, tiles, stride):
    def move(step, carry):
        for lane in range(SUBLANES):
            base = index_ref[first + step * SUBLANES + lane]
            target[pl.ds(step * SUBLANES * tiles + lane, tiles, stride=SUBLANES), :] = source[
                pl.ds(base, tiles, stride=stride), :
            ]
        return carry

    lax.fori_loop(0, count // SUBLANES, move, 0, unroll=4)


def from_view(value, rows, tiles):
    shaped = value.reshape(rows // SUBLANES, tiles, SUBLANES, LANES)
    return jnp.concatenate([shaped[:, t].reshape(rows, LANES) for t in range(tiles)], axis=1)


def pack_kernel(rows, tiles, index_ref, source_hbm, onehot_ref, *refs):
    outs, (held, picked, sem) = refs[:-3], refs[-3:]
    step = pl.program_id(0)

    @pl.when(step == 0)
    def _():
        size = source_hbm.shape[0]
        copy = pltpu.make_async_copy(source_hbm, held.at[pl.ds(0, size)], sem)
        copy.start()
        copy.wait()

    copy_rows(index_ref, step * rows, held, picked, rows, tiles, SUBLANES)
    high, low = split(from_view(picked[: rows * tiles], rows, tiles))
    places = [(out, None) for out in outs]
    if len(outs) == 1:
        places = [(outs[0], d) for d in range(outs[0].shape[1])]
    lanes = onehot_ref.shape[2]
    if lanes % LANES == 0:
        whole = jnp.concatenate([onehot_ref[d] for d in range(len(places))], axis=1)
        moved = product(high, whole) + product(low, whole)
        parts = [moved[:, d * lanes : (d + 1) * lanes] for d in range(len(places))]
    else:
        parts = [
            product(high, onehot_ref[d]) + product(low, onehot_ref[d]) for d in range(len(places))
        ]
    for part, (out, d) in zip(parts, places):
        if d is None:
            out[...] = part.reshape(out.shape)
        else:
            out[:, d] = part.reshape(out.shape[0], out.shape[2], lanes)


def pack(view, bases, onehot, row_devices, width, apart):
    col_devices, cols, group = onehot.shape
    tiles = cols // LANES
    groups = group_step(row_devices, width)
    rows = groups * width
    if apart:
        shapes = [jax.ShapeDtypeStruct((row_devices, width, group), jnp.float32)] * col_devices
        specs = [pl.BlockSpec((groups, width, group), lambda i: (i, 0, 0))] * col_devices
    else:
        shapes = [jax.ShapeDtypeStruct((row_devices, col_devices, width, group), jnp.float32)]
        specs = [pl.BlockSpec((groups, col_devices, width, group), lambda i: (i, 0, 0, 0))]
    return pl.pallas_call(
        functools.partial(pack_kernel, rows, tiles),
        out_shape=shapes,
        grid=(row_devices // groups,),
        in_specs=[
            pl.BlockSpec(memory_space=pltpu.SMEM),
            pl.BlockSpec(memory_space=pl.ANY),
            pl.BlockSpec(onehot.shape, lambda i: (0, 0, 0)),
        ],
        out_specs=specs,
        scratch_shapes=[
            pltpu.VMEM((view.shape[0] + SUBLANES * tiles, LANES), jnp.float32),
            pltpu.VMEM((rows * tiles + SUBLANES * tiles, LANES), jnp.float32),
            pltpu.SemaphoreType.DMA,
        ],
        compiler_params=pltpu.CompilerParams(vmem_limit_bytes=VMEM_LIMIT),
        cost_estimate=LIGHT,
        name="pack",
    )(bases, view, onehot)


def place_columns(pieces, onehot_ref, rows):
    if len(pieces[0].shape) == 4:
        pieces = [pieces[0][:, c] for c in range(pieces[0].shape[1])]
    values = [piece[...].reshape(rows, piece.shape[-1]) for piece in pieces]
    if values[0].shape[1] % LANES == 0:
        high, low = split(jnp.concatenate(values, axis=1))
        whole = onehot_ref[...].reshape(high.shape[1], onehot_ref.shape[2])
        return product(high, whole) + product(low, whole)
    total = None
    for d, value in enumerate(values):
        high, low = split(value)
        part = product(high, onehot_ref[d]) + product(low, onehot_ref[d])
        total = part if total is None else total + part
    return total


def mix_kernel(rows, counts, onehot_ref, *refs):
    pieces, outs = refs[: -len(counts)], refs[-len(counts) :]
    moved = place_columns(pieces, onehot_ref, rows)
    tile = 0
    for count, out in zip(counts, outs):
        for t in range(count):
            part = moved[:, (tile + t) * LANES : (tile + t + 1) * LANES]
            out[:, t] = part.reshape(out.shape[0], out.shape[2], LANES)
        tile += count


def mix(pieces, onehot, counts):
    row_devices, width, lanes = pieces[0].shape
    groups = group_step(row_devices, width)
    rows = groups * width
    return pl.pallas_call(
        functools.partial(mix_kernel, rows, counts),
        out_shape=[
            jax.ShapeDtypeStruct((row_devices, count, width, LANES), jnp.float32) for count in counts
        ],
        grid=(row_devices // groups,),
        in_specs=[pl.BlockSpec(onehot.shape, lambda i: (0, 0, 0))]
        + [pl.BlockSpec((groups, width, lanes), lambda i: (i, 0, 0))] * len(pieces),
        out_specs=[
            pl.BlockSpec((groups, count, width, LANES), lambda i: (i, 0, 0, 0)) for count in counts
        ],
        compiler_params=pltpu.CompilerParams(vmem_limit_bytes=VMEM_LIMIT),
        cost_estimate=LIGHT,
        name="mix",
    )(onehot, *pieces)


def goce_rows_kernel(rows, index_ref, weight_ref, goce_hbm, out_ref, held, picked, sem):
    step = pl.program_id(0)

    @pl.when(step == 0)
    def _():
        copy = pltpu.make_async_copy(goce_hbm.at[:, pl.ds(0, BLOCK)], held, sem)
        copy.start()
        copy.wait()

    copy_rows(index_ref, step * rows, held, picked, rows, 1, 1)
    out_ref[...] = weight_ref[1] * picked[:rows]


def goce_rows(places, weights, goce, row_devices):
    total = places.shape[0]
    rows = total // row_devices * group_step(row_devices, total // row_devices)
    return pl.pallas_call(
        functools.partial(goce_rows_kernel, rows),
        out_shape=jax.ShapeDtypeStruct((total, BLOCK), jnp.float32),
        grid=(total // rows,),
        in_specs=[
            pl.BlockSpec(memory_space=pltpu.SMEM),
            pl.BlockSpec(memory_space=pltpu.SMEM),
            pl.BlockSpec(memory_space=pl.ANY),
        ],
        out_specs=pl.BlockSpec((rows, BLOCK), lambda i: (i, 0)),
        scratch_shapes=[
            pltpu.VMEM((goce.shape[0], BLOCK), jnp.float32),
            pltpu.VMEM((rows + SUBLANES, BLOCK), jnp.float32),
            pltpu.SemaphoreType.DMA,
        ],
        compiler_params=pltpu.CompilerParams(vmem_limit_bytes=VMEM_LIMIT),
        cost_estimate=LIGHT,
        name="goce_rows",
    )(places, weights, goce)


def panel_kernel(rows, weight_ref, added_ref, onehot_ref, received_ref, out_ref):
    moved = place_columns([received_ref], onehot_ref, rows)
    out_ref[...] = weight_ref[0] * moved + added_ref[...]


def panel_part(received, added, weights, onehot):
    row_devices, width = received.shape[0], received.shape[2]
    groups = group_step(row_devices, width)
    rows = groups * width
    return pl.pallas_call(
        functools.partial(panel_kernel, rows),
        out_shape=jax.ShapeDtypeStruct((row_devices * width, BLOCK), jnp.float32),
        grid=(row_devices // groups,),
        in_specs=[
            pl.BlockSpec(memory_space=pltpu.SMEM),
            pl.BlockSpec((rows, BLOCK), lambda i: (i, 0)),
            pl.BlockSpec(onehot.shape, lambda i: (0, 0, 0)),
            pl.BlockSpec((groups,) + received.shape[1:], lambda i: (i, 0, 0, 0)),
        ],
        out_specs=pl.BlockSpec((rows, BLOCK), lambda i: (i, 0)),
        compiler_params=pltpu.CompilerParams(vmem_limit_bytes=VMEM_LIMIT),
        cost_estimate=HEAVY,
        name="panel",
    )(weights, added, onehot, received)


def update_kernel(rows, placed, parts, weight_ref, mask_ref, keep_ref, high_ref, low_ref, *refs):
    step = pl.program_id(0)
    raw_count = sum(count for _, _, count in parts)
    raws, arrays, out_ref = refs[:raw_count], refs[raw_count:-1], refs[-1]

    def compute(pieces):
        raw = jnp.concatenate(pieces, axis=1)
        if not placed:
            raw = raw * keep_ref[...]
        high, low = split(raw)
        total = product(high, high_ref[...]) + product(low, high_ref[...])
        total = total + product(high, low_ref[...])
        if placed:
            shape = arrays[0].shape
            tiles = [arrays[0][:, t].reshape(rows, LANES) for t in range(shape[1])]
        else:
            moved = place_columns(arrays[1:], arrays[0], rows)
            tiles = [moved[:, t * LANES : (t + 1) * LANES] for t in range(moved.shape[1] // LANES)]
        for t in range(total.shape[1] // LANES):
            lanes = slice(t * LANES, (t + 1) * LANES)
            part = total[:, lanes]
            if t < len(tiles):
                part = part + (weight_ref[0] * mask_ref[:, lanes]) * tiles[t]
            out_ref[:, t] = part.reshape(rows // SUBLANES, SUBLANES, LANES)

    used = 0
    for first, steps, count in parts:
        mine = raws[used : used + count]
        used += count

        @pl.when((step >= first) & (step < first + steps))
        def _():
            if count == 1:
                compute([mine[0][p] for p in range(high_ref.shape[0] // BLOCK)])
            else:
                compute([ref[...] for ref in mine])


def part_map(first, steps, step):
    return (jnp.clip(step - first, 0, steps - 1), 0)


def update_part(arrays, raw, keep, weights, mask, onehot, high, low):
    placed = onehot is None
    row_devices, width, lanes = arrays[0].shape[0], arrays[0].shape[-2], arrays[0].shape[-1]
    cols = high.shape[1]
    tiles = cols // LANES
    groups = group_step(row_devices, width)
    rows = groups * width
    total = row_devices * width
    if isinstance(raw, list):
        parts, raw_specs, flat, first = [], [], [], 0
        for pieces in raw:
            steps = pieces[0].shape[0] // rows
            parts.append((first, steps, len(pieces)))
            place = functools.partial(part_map, first, steps)
            raw_specs += [pl.BlockSpec((rows, BLOCK), place)] * len(pieces)
            flat += pieces
            first += steps
    else:
        parts = [(0, row_devices // groups, 1)]
        raw_specs = [pl.BlockSpec((high.shape[0] // BLOCK, rows, BLOCK), lambda i: (0, i, 0))]
        flat = [raw]
    if placed:
        specs = [pl.BlockSpec((groups,) + arrays[0].shape[1:], lambda i: (i, 0, 0, 0))]
    else:
        specs = [pl.BlockSpec((groups,) + arrays[0].shape[1:], lambda i: (i, 0, 0, 0))]
        specs = [pl.BlockSpec(onehot.shape, lambda i: (0, 0, 0))] + specs
        arrays = [onehot] + list(arrays)
    return pl.pallas_call(
        functools.partial(update_kernel, rows, placed, tuple(parts)),
        out_shape=jax.ShapeDtypeStruct((total // SUBLANES, tiles, SUBLANES, LANES), jnp.float32),
        grid=(row_devices // groups,),
        in_specs=[
            pl.BlockSpec(memory_space=pltpu.SMEM),
            pl.BlockSpec((1, cols), lambda i: (0, 0)),
            pl.BlockSpec((rows if not placed else SUBLANES, 1), lambda i: (0 if placed else i, 0)),
            pl.BlockSpec(high.shape, lambda i: (0, 0)),
            pl.BlockSpec(low.shape, lambda i: (0, 0)),
        ]
        + raw_specs
        + specs,
        out_specs=pl.BlockSpec((rows // SUBLANES, tiles, SUBLANES, LANES), lambda i: (i, 0, 0, 0)),
        compiler_params=pltpu.CompilerParams(vmem_limit_bytes=VMEM_LIMIT),
        cost_estimate=LIGHT,
        name="update",
    )(weights, mask, keep, high, low, *flat, *arrays).reshape(-1, LANES)


def finish_kernel(rows, tiles, lane, stride, weighted, has_head, bounds_ref, index_ref, weight_ref, part_hbm, head_ref, base_hbm, out_hbm, held, picked, before, after, part_sem, in_sem, out_sem):
    size = part_hbm.shape[0]
    first, last = bounds_ref[0], bounds_ref[1]
    for source in range(1, bounds_ref.shape[0] // 2):
        first = jnp.minimum(first, bounds_ref[2 * source])
        last = jnp.maximum(last, bounds_ref[2 * source + 1])
    first = first // rows
    steps = last // rows + 1 - first
    lanes = pl.ds(lane, tiles * LANES)

    def block(step):
        return pl.ds(pl.multiple_of((first + step) * rows, rows), rows)

    def fetch(step, slot):
        return pltpu.make_async_copy(out_hbm.at[block(step), lanes], before.at[slot], in_sem.at[slot])

    def store(step, slot):
        return pltpu.make_async_copy(after.at[slot], out_hbm.at[block(step), lanes], out_sem.at[slot])

    part_copy = pltpu.make_async_copy(part_hbm, held.at[pl.ds(0, size)], part_sem)
    part_copy.start()
    fetch(0, 0).start()
    held[pl.ds(size, held.shape[0] - size), :] = jnp.zeros((held.shape[0] - size, LANES), jnp.float32)
    part_copy.wait()

    def body(step, carry):
        slot = lax.rem(step, 2)

        @pl.when(step + 1 < steps)
        def _():
            fetch(step + 1, 1 - slot).start()

        copy_rows(index_ref, (first + step) * rows, held, picked, rows, tiles, stride)
        fetch(step, slot).wait()

        @pl.when(step >= 2)
        def _():
            store(step - 2, slot).wait()

        added = from_view(picked[: rows * tiles], rows, tiles)
        if weighted:
            added = weight_ref[0] * added
        after[slot] = before[slot] + added
        if has_head:

            @pl.when(step == 0)
            def _():
                count = head_ref.shape[0]
                after[0, :count] = after[0, :count] + head_ref[...]

        store(step, slot).start()
        return carry

    lax.fori_loop(0, steps, body, 0)

    @pl.when(steps >= 2)
    def _():
        store(steps - 2, lax.rem(steps, 2)).wait()

    store(steps - 1, lax.rem(steps + 1, 2)).wait()


def finish_index(local, count, tiles, width):
    index, size = view_base(local, tiles), count * tiles
    if width:
        index = local // width * (width * (tiles - 1)) + local % width
        size = count * (tiles - 1)
    return jnp.where((local >= 0) & (local < count), index, size)


def finish_part(base, part, bounds, index, weights, head, width, has_head):
    total, cols = base.shape
    tiles = cols // LANES
    rows = head.shape[0]
    while rows < 512 and total % (2 * rows) == 0:
        rows *= 2
    lane, stride = 0, SUBLANES
    if width:
        tiles -= 1
        lane, stride = LANES, width
    spare = stride * tiles + SUBLANES
    return pl.pallas_call(
        functools.partial(finish_kernel, rows, tiles, lane, stride, bool(width), has_head),
        out_shape=jax.ShapeDtypeStruct((total, cols), jnp.float32),
        in_specs=[
            pl.BlockSpec(memory_space=pltpu.SMEM),
            pl.BlockSpec(memory_space=pltpu.SMEM),
            pl.BlockSpec(memory_space=pltpu.SMEM),
            pl.BlockSpec(memory_space=pl.ANY),
            pl.BlockSpec(memory_space=pltpu.VMEM),
            pl.BlockSpec(memory_space=pl.ANY),
        ],
        out_specs=pl.BlockSpec(memory_space=pl.ANY),
        scratch_shapes=[
            pltpu.VMEM((part.shape[0] + spare, LANES), jnp.float32),
            pltpu.VMEM((rows * tiles + SUBLANES * tiles, LANES), jnp.float32),
            pltpu.VMEM((2, rows, tiles * LANES), jnp.float32),
            pltpu.VMEM((2, rows, tiles * LANES), jnp.float32),
            pltpu.SemaphoreType.DMA,
            pltpu.SemaphoreType.DMA((2,)),
            pltpu.SemaphoreType.DMA((2,)),
        ],
        input_output_aliases={5: 0},
        compiler_params=pltpu.CompilerParams(vmem_limit_bytes=VMEM_LIMIT),
        cost_estimate=LIGHT,
        name="finish",
    )(bounds, index, weights, part, head, base)


def precise(left, right):
    return jnp.dot(left, right, precision=lax.Precision.HIGHEST)


def cholesky_inverse(blocks, pause):
    count = len(blocks)
    size = blocks[0][0].shape[0]
    identity = jnp.eye(size, dtype=jnp.float32)
    factor, inverse = {}, {}
    for b in range(count):
        pivot = jnp.tril(blocks[b][b]) + jnp.tril(blocks[b][b], -1).T
        if b:
            left = jnp.concatenate([factor[b, k] for k in range(b)], axis=1)
            pivot = pivot - precise(left, left.T)
        factor[b, b] = jnp.linalg.cholesky(pivot, symmetrize_input=False)
        inverse[b, b] = jax.scipy.linalg.solve_triangular(factor[b, b], identity, lower=True)
        if b + 1 < count:
            below = jnp.concatenate([blocks[i][b] for i in range(b + 1, count)], axis=0)
            if b:
                rows = [
                    jnp.concatenate([factor[i, k] for k in range(b)], axis=1)
                    for i in range(b + 1, count)
                ]
                below = below - precise(jnp.concatenate(rows, axis=0), left.T)
            below = pause(b, precise(below, inverse[b, b].T))
            for i in range(b + 1, count):
                factor[i, b] = below[(i - b - 1) * size : (i - b) * size]
    zero = jnp.zeros((size, size), jnp.float32)
    for b in range(1, count):
        left = jnp.concatenate([factor[b, k] for k in range(b)], axis=1)
        above = [
            jnp.concatenate([inverse[k, j] if k >= j else zero for j in range(b)], axis=1)
            for k in range(b)
        ]
        solved = -precise(inverse[b, b], precise(left, jnp.concatenate(above, axis=0)))
        for j in range(b):
            inverse[b, j] = solved[:, j * size : (j + 1) * size]
    whole = [
        [
            jnp.concatenate([part[i, j] if i >= j else zero for j in range(count)], axis=1)
            for i in range(count)
        ]
        for part in (factor, inverse)
    ]
    return jnp.concatenate(whole[0], axis=0), jnp.concatenate(whole[1], axis=0)


def shards(
    grace_slab, goce_slab, grace_weight, goce_weight, kaula_prior, row_target, column_target
):
    row_devices = lax.axis_size("prow")
    col_devices = lax.axis_size("pcol")
    row_id = lax.axis_index("prow")
    col_id = lax.axis_index("pcol")
    rows_here, cols_here = grace_slab.shape
    tiles = cols_here // LANES
    row_group = rows_here // row_devices
    col_group = cols_here // col_devices
    per_device = SLAB // (BLOCK * row_devices)
    lead = per_device * BLOCK
    widths = chunk_widths(row_group, lead)
    starts = [sum(widths[:n]) for n in range(len(widths))]
    counts = [row_devices * width for width in widths]
    weights = jnp.concatenate([grace_weight, goce_weight])
    tie = lax.optimization_barrier

    bits = (rows_here - 1).bit_length()
    mask = (1 << bits) - 1
    local = jnp.arange(rows_here, dtype=jnp.int32)
    mine = lax.dynamic_slice_in_dim(row_target, row_id * rows_here, rows_here)
    sources = (jnp.sort(mine * (1 << bits) + local) & mask).reshape(row_devices, row_group)
    source_bases = view_base(sources, tiles)
    chunk_bases = [
        source_bases[:, start : start + width].reshape(-1) for start, width in zip(starts, widths)
    ]
    my_cols = lax.dynamic_slice_in_dim(column_target, col_id * cols_here, cols_here)
    col_ranks = jnp.sum((my_cols[None, :] < my_cols[:, None]).astype(jnp.int32), axis=1)
    distance = jnp.arange(col_devices, dtype=jnp.int32)
    group_iota = jnp.arange(col_group, dtype=jnp.int32)

    def column_onehot(owners):
        return (
            ((col_ranks // col_group)[None, :, None] == owners[:, None, None])
            & ((col_ranks % col_group)[None, :, None] == group_iota[None, None, :])
        ).astype(jnp.bfloat16)

    whole_onehot = column_onehot(distance)
    send_onehot = column_onehot(distance ^ col_id)

    def exchange(packet, axes, devices):
        sent = packet.reshape(devices, -1, packet.shape[-1])
        got = lax.all_to_all(sent, axes, split_axis=0, concat_axis=0, tiled=True)
        return got.reshape(packet.shape)

    def over_rows(packet):
        return exchange(packet, "prow", row_devices)

    def over_cols(pieces):
        got = [pieces[0]]
        for d in range(1, col_devices):
            pairs = [(i, i ^ d) for i in range(col_devices)]
            got.append(lax.ppermute(pieces[d], "pcol", pairs))
        return got

    view = row_view(grace_slab)
    (packet,) = pack(view, chunk_bases[0], whole_onehot, row_devices, widths[0], False)
    first_got = exchange(packet, ("prow", "pcol"), row_devices * col_devices)
    (chunk_bases[1], packet) = tie((chunk_bases[1], packet))
    second = over_cols(pack(view, chunk_bases[1], send_onehot, row_devices, widths[1], True))
    third = pack(view, chunk_bases[2], send_onehot, row_devices, widths[2], True)

    sorted_rows = jnp.sort(row_target.reshape(row_devices, rows_here), axis=1)
    places = lax.dynamic_slice_in_dim(sorted_rows, row_id * row_group, row_group, axis=1)
    places = places - row_id * rows_here
    chunk_places = [
        places[:, start : start + width].reshape(-1) for start, width in zip(starts, widths)
    ]
    ends = [
        jnp.stack([places[:, start], places[:, start + width - 1]], axis=-1).reshape(-1)
        for start, width in zip(starts, widths)
    ]
    positions = jnp.sort(jnp.concatenate(chunk_places) * (1 << bits) + local) & mask
    sorted_cols = jnp.sort(column_target.reshape(col_devices, cols_here), axis=1)
    col_targets = lax.dynamic_slice_in_dim(sorted_cols, col_id * col_group, col_group, axis=1)
    col_targets = col_targets - col_id * cols_here
    col_iota = jnp.arange(cols_here, dtype=jnp.int32)
    take_whole = (col_targets[:, :, None] == col_iota[None, None, :]).astype(jnp.bfloat16)
    take_onehot = jnp.take(take_whole, distance ^ col_id, axis=0)
    order_cols = order_index(cols_here, col_id, col_devices, BLOCK)
    in_panel = order_cols < PANEL
    outside = jnp.where(in_panel, 0.0, 1.0)[None, :].astype(jnp.float32)
    out = goce_slab * (goce_weight[0] * outside)

    first = chunk_places[0]
    first_order = (first // BLOCK * row_devices + row_id) * BLOCK + first % BLOCK
    keep = jnp.where(first_order < PANEL, 0.0, 1.0)[:, None].astype(jnp.float32)

    offsets = [sum(counts[:n]) for n in range(len(counts))]
    indices = [
        finish_index(positions - offset, count, tiles, 0) for offset, count in zip(offsets, counts)
    ]
    indices.append(finish_index(positions - offsets[-1], counts[-1], tiles, widths[-1]))
    added = [goce_rows(where, weights, goce_slab, row_devices) for where in chunk_places]

    second, third, added, ends, positions, take_onehot, take_whole, out, keep, indices = tie(
        (second, third, added, ends, positions, take_onehot, take_whole, out, keep, indices)
    )
    third = over_cols(third)
    (second_packet,) = mix(second, take_onehot, (tiles,))
    second_packet, first_got = tie((second_packet, first_got))
    second_got = over_rows(second_packet)
    panels = [panel_part(first_got, added[0], weights, take_whole[:, :, :BLOCK])]
    panel_blocks = PANEL // BLOCK
    my_lead = jnp.take(panels[0], positions[:lead], axis=0).reshape(per_device, BLOCK, BLOCK)
    lead_order = jnp.arange(per_device, dtype=jnp.int32) * row_devices + row_id
    my_diag = jnp.where(lead_order[:, None] == col_id, kaula_prior[None, :BLOCK], 0.0)
    my_lead = my_lead + my_diag[:, :, None] * jnp.eye(BLOCK, dtype=jnp.float32)
    lead_cols = lax.all_gather(my_lead, "prow", axis=0)
    lead_cols = lead_cols.transpose(1, 0, 2, 3).reshape(-1, BLOCK, BLOCK)
    outer = [n for n in range(tiles) if (n + 1) * col_devices > panel_blocks]
    lead_parts = []
    for d in range(col_devices):
        wanted = jnp.array(outer, dtype=jnp.int32) * col_devices + (col_id ^ d)
        lead_parts.append(
            jnp.concatenate([lead_cols[:panel_blocks], jnp.take(lead_cols, wanted, axis=0)], axis=0)
        )
    lead_all = jnp.take(jnp.stack(over_cols(lead_parts)), distance ^ col_id, axis=0)[:panel_blocks]

    third_packets = list(mix(third, take_onehot, (1, tiles - 1)))
    lead_all, third_packets = tie((lead_all, third_packets))
    blocks = [[lead_all[j, i] for j in range(i + 1)] for i in range(panel_blocks)]
    late = {}

    def pause(step, value):
        if step == 0:
            value, late["second"], packet = tie((value, second_got, third_packets[0]))
            late["panel"] = over_rows(packet)
        if step == min(REST_STEP, panel_blocks - 2):
            value, late["panel"], packet = tie((value, late["panel"], third_packets[1]))
            late["rest"] = over_rows(packet)
        return value

    factor, inverse = cholesky_inverse(blocks, pause)
    second_got, third_panel, third_rest = late["second"], late["panel"], late["rest"]
    col_rows = []
    for n in range(tiles):
        if n in outer:
            rows = lead_all[:, panel_blocks + outer.index(n)]
            col_rows.append(rows.transpose(1, 0, 2).reshape(BLOCK, PANEL))
        else:
            col_rows.append(jnp.zeros((BLOCK, PANEL), jnp.float32))
    col_rows = jnp.concatenate(col_rows, axis=0)
    solved = precise(inverse, col_rows.T)
    panel_iota = jnp.arange(PANEL, dtype=jnp.int32)
    identity = (panel_iota[:, None] == order_cols[None, :]).astype(jnp.float32)
    matrix = precise(inverse.T, jnp.where(in_panel[None, :], identity, -solved))
    matrix_high, matrix_low = split_array(matrix)

    order_rows = order_index(lead, row_id, row_devices, BLOCK)
    on_diagonal = order_rows[:, None] == order_cols[None, :]
    known = jnp.take(
        jnp.take(factor, jnp.minimum(order_rows, PANEL - 1), axis=0),
        jnp.minimum(order_cols, PANEL - 1),
        axis=1,
    )
    in_block = (order_rows[:, None] < PANEL) & in_panel[None, :]
    head = jnp.where(in_block, known, jnp.where(on_diagonal, kaula_prior[None, :], 0.0))
    panels[0], third = tie((panels[0], third))
    for n, got in ((1, second_got), (2, third_panel)):
        panels.append(grace_weight[0] * got[:, 0].reshape(-1, BLOCK) + added[n])
    raws = [lax.all_gather(panel, "pcol", axis=0) for panel in panels]
    arrays = [[first_got], [second_got], [third_panel]]
    for n in range(len(widths)):
        part = update_part(
            arrays[n],
            raws[n],
            keep,
            weights,
            outside,
            take_whole if n == 0 else None,
            matrix_high,
            matrix_low,
        )
        out = finish_part(out, part, ends[n], indices[n], weights, head, 0, n == 0)
    out, third_rest = tie((out, third_rest))
    rest_rows = third_rest.reshape(-1, LANES)
    return finish_part(out, rest_rows, ends[-1], indices[-1], weights, head, widths[-1], False)


def solution(mesh):
    return jax.shard_map(
        shards,
        mesh=mesh,
        in_specs=(P("prow", "pcol"), P("prow", "pcol"), P(), P(), P("pcol"), P(), P()),
        out_specs=P("prow", "pcol"),
        check_vma=False,
    )
```
